256 devices in a mesh: fsdp: 32 (over x_hi, z, core), tensor: 8 (over x_lo, y).
Axes of the slice: x: 4 (x_hi: 2, x_lo: 2; x = x_hi * 2 + x_lo), y: 4, z: 8, core: 2. Of those that a mesh axis runs over, the one named last changes fastest.
Arguments:
- gate_pre: bfloat16 [4096, 14336], P('fsdp', 'tensor'), may hold values from -6 to 6
- up_pre: bfloat16 [4096, 14336], P('fsdp', 'tensor'), may hold values from -6 to 6
- down_weight: bfloat16 [14336, 4096], P('tensor', 'fsdp'), may hold values from -0.046875 to 0.046875
- residual: bfloat16 [4096, 4096], P('fsdp'), may hold values from -6 to 6
- target_rows: bfloat16 [4096, 4096], P('fsdp'), may hold values from -0.1875 to 0.1875
- loss_mask: int32 [4096], P('fsdp'), may hold values 0 or 1
- response_count: int32 [64], P('fsdp'), may hold values from 32 to 64
Outputs:
- pair_loss: float32 [32], P('fsdp')
- grad_gate: bfloat16 [4096, 14336], P('fsdp', 'tensor')
- grad_up: bfloat16 [4096, 14336], P('fsdp', 'tensor')
- grad_down: float32 [14336, 4096], P('tensor', 'fsdp')
The draws below stay inside these ranges and needn't reach their ends.
All inputs are finite; a program needn't handle non-finite values. No bound on the sum of `loss_mask` on one device may be relied on, other than what follows from the above.
Results may differ from the reference program's by a relative error of at most 0.025.
Values may be sent and summed in bfloat16 or wider, within the bound.
A program may use at most 128 MiB of HBM per device.

```python
import jax
import jax.numpy as jnp
from jax import lax

D = 4096
FF = 14336
L = 64
TOK_GRP = 128
TOKENS = 4096
SEQS = 64
PAIRS = 32
N_FSDP = 32


def touch_ends(entries, rng, low, top_value):
    extent = entries.shape
    place = [jax.random.randint(jax.random.fold_in(rng, axis), (), 0, extent[axis]) for axis in range(len(extent))]
    entries = entries.at[tuple(place)].set(low)
    longest = extent.index(max(extent))
    place[longest] = (place[longest] + 1) % extent[longest]
    return entries.at[tuple(place)].set(top_value)


def spiked(values, key, source, target, blocks, factor):
    def block_of(axis_at):
        return (jnp.arange(values.shape[axis_at]) // (values.shape[axis_at] // blocks)).reshape((-1,) + (1,) * (values.ndim - 1 - axis_at))

    one_side = jax.random.permutation(key, blocks)[block_of(target)]
    other_side = (block_of(target) + blocks // 2) % blocks
    return jnp.where((block_of(source) == one_side) | (block_of(source) == other_side), factor * values, values)


def level_of(stream_key, extent, split, low, high):
    factor_of = 1.0
    for position, blocks in split:
        draws = jax.random.uniform(jax.random.fold_in(jax.random.fold_in(stream_key, 6), position), (blocks,), jnp.float32, low / len(split), high / len(split))
        factor_of = factor_of * jnp.repeat(jnp.exp(draws), extent[position] // blocks).reshape((-1,) + (1,) * (len(extent) - 1 - position))
    return factor_of


def bell_draw(key, shape, deviation, reach, cuts=(), kind=jnp.bfloat16):
    values = deviation * jax.random.normal(key, shape, jnp.float32)
    if cuts:
        values = values * level_of(key, shape, cuts, -0.22, 0.18)
    return jnp.clip(values, -reach, reach).astype(kind)


def heavy_noise(stream_key, extent, deviation, limit, shards, heavy, dtype=jnp.bfloat16):
    values = deviation * jax.random.normal(stream_key, extent, jnp.float32)
    if shards:
        values = values * level_of(stream_key, extent, shards, -0.22, 0.18)
    return jnp.clip(spiked(values, jax.random.fold_in(stream_key, 3), *heavy), -limit, limit).astype(dtype)


def setup_inputs(seed: int = 0) -> dict:
    key_of = jax.random.split(jax.random.key(seed), 8)
    gate_pre = bell_draw(key_of[0], (TOKENS, FF), 1.0, 6.0, ((0, 32), (1, 8)))
    up_pre = bell_draw(key_of[1], (TOKENS, FF), 1.0, 6.0, ((0, 32), (1, 8)))
    down_weight = bell_draw(key_of[2], (FF, D), FF ** -0.5, 0.046875, ((0, 8), (1, 32)))
    residual = bell_draw(key_of[3], (TOKENS, D), 1.0, 6.0, ((0, 32),))
    target_rows = heavy_noise(key_of[4], (TOKENS, D), D ** -0.5, 0.1875, ((0, 32),), (0, 1, 32, 2.75))
    loss_mask = touch_ends((jax.random.randint(key_of[5], (TOKENS,), 0, 4) < 3).astype(jnp.int32), jax.random.fold_in(key_of[5], 1), 0, 1)
    response_count = touch_ends(jax.random.randint(key_of[6], (SEQS,), L // 2, L + 1), jax.random.fold_in(key_of[6], 1), L // 2, L).astype(jnp.int32)
    return {"gate_pre": gate_pre, "up_pre": up_pre, "down_weight": down_weight, "residual": residual, "target_rows": target_rows, "loss_mask": loss_mask, "response_count": response_count}


beta_coef = 2.0
gamma_margin = 1.0
loss_scale = 1024.0


def reference(gate_pre, up_pre, down_weight, residual, target_rows, loss_mask, response_count):
    gate_wide = gate_pre.astype(jnp.float32)
    up_wide = up_pre.astype(jnp.float32)
    gate_sigmoid = jax.nn.sigmoid(gate_wide)
    hidden = (gate_wide * gate_sigmoid * up_wide).astype(jnp.bfloat16)
    block = residual.astype(jnp.float32) + jnp.dot(hidden, down_weight, preferred_element_type=jnp.float32)
    scores = jnp.sum(block * target_rows.astype(jnp.float32), axis=1)
    mask_float = loss_mask.astype(jnp.float32)
    seq_sums = jnp.sum((scores * mask_float).reshape(SEQS, L), axis=1)
    counts = response_count.astype(jnp.float32)
    rewards = beta_coef * seq_sums / counts
    paired = rewards.reshape(PAIRS, 2)
    margin = paired[:, 0] - paired[:, 1] - gamma_margin
    pair_loss = jax.nn.softplus(-margin)
    weight = jax.nn.sigmoid(-margin) * loss_scale * beta_coef
    signs = jnp.array([-1.0, 1.0], jnp.float32)
    seq_factor = (weight[:, None] * signs[None, :]).reshape(SEQS) / counts
    token_factor = jnp.repeat(seq_factor, L) * mask_float
    back = jnp.dot(target_rows, down_weight.T, preferred_element_type=jnp.float32)
    grad_hidden = token_factor[:, None] * back
    slope = gate_sigmoid + gate_wide * gate_sigmoid * (1.0 - gate_sigmoid)
    grad_gate = (grad_hidden * up_wide * slope).astype(jnp.bfloat16)
    grad_up = (grad_hidden * gate_wide * gate_sigmoid).astype(jnp.bfloat16)
    scaled = (token_factor[:, None] * hidden.astype(jnp.float32)).astype(jnp.bfloat16)
    scaled_groups = scaled.reshape(N_FSDP, TOK_GRP, FF)
    target_groups = target_rows.reshape(N_FSDP, TOK_GRP, D)

    def add_group(total, pieces):
        term = jnp.dot(pieces[0].T, pieces[1], preferred_element_type=jnp.float32)
        rounded = lax.optimization_barrier(term.astype(jnp.bfloat16))
        return total + rounded.astype(jnp.float32), None

    grad_down, _ = lax.scan(add_group, jnp.zeros((FF, D), jnp.float32), (scaled_groups, target_groups))
    return pair_loss, grad_gate, grad_up, grad_down
```

```python
import functools

import jax
import jax.numpy as jnp
from jax import lax
from jax.experimental import pallas as pl
from jax.experimental.pallas import tpu as pltpu
from jax.sharding import PartitionSpec as P

MESH = pl.DeviceIdType.MESH
F32 = jnp.float32
BF16 = jnp.bfloat16

beta_coef = 2.0
gamma_margin = 1.0
loss_scale = 1024.0

L = 64
NZ = 8
TOK = 128
COL = 128
UNIT = 256
NU = 7
HID = UNIT * NU
D = 4096

W_GROUPS = (((0, 512), (512, 512)), ((1024, 384), (1408, 384)))
H_GROUPS = ((0, 2, 0), (2, 2, 1), (4, 2, 2), (6, 1, 3))
STEPS = NZ - 1


def kernel(
    gate, up, w, resid, tgt, mask, cnt, loss, gg, gu, gd,
    gv, uv, rv, tv, tp, t1, t2, t2t, t2s, wg, hg, pm, cs, cr, xs, xr, bk,
    dm, cs2, cr2, xs2, xr2, ggv, guv, gdv, sb, fg,
    ld_sem, out_sem, ws, wr, hs, hr, t1s, t1r, t2as, t2ar, t2gs, t2gr,
    css, crs, xss, xrs, css2, crs2, xss2, xrs2, sbs, sbr, fgs, fgr,
):
    f = lax.axis_index("fsdp")
    g = lax.axis_index("tensor")
    xh, z, c = f // 16, (f // 2) % 8, f % 2
    xl, y = g // 4, g % 4

    def place(xh_, z_, c_, xl_=xl, y_=y):
        return (xh_ * 16 + z_ * 2 + c_, xl_ * 4 + y_)

    def z_at(k):
        return (f // 16 * 16 + (z + k) % 8 * 2 + c, g)

    def g_at(k):
        return (f, (g + k) % 8)

    core = place(xh, z, 1 - c)
    xopp = place(1 - xh, z, c)
    xnb = (place(1 - xh, z, c, 1 - xl), place(1 - xh, z, 1 - c, 1 - xl))
    ahead, behind = z_at(1), z_at(7)

    loads = [
        pltpu.make_async_copy(tgt, tv, ld_sem.at[0]),
        pltpu.make_async_copy(w, wg.at[z], ld_sem.at[1]),
        pltpu.make_async_copy(gate, gv, ld_sem.at[2]),
        pltpu.make_async_copy(up, uv, ld_sem.at[3]),
        pltpu.make_async_copy(
            resid.at[:, pl.ds(pl.multiple_of(g * 512, 512), 512)], rv, ld_sem.at[4]
        ),
    ]
    for load in loads:
        load.start()

    barrier = pltpu.get_barrier_semaphore()
    partners = [z_at(k) for k in range(1, 8)] + [g_at(k) for k in range(1, 8)]
    partners += [core, xopp, *xnb]
    for partner in partners:
        pl.semaphore_signal(barrier, inc=1, device_id=partner, device_id_type=MESH)

    def remote(src, dst, ssem, rsem, device):
        return pltpu.make_async_remote_copy(
            src_ref=src, dst_ref=dst, send_sem=ssem, recv_sem=rsem,
            device_id=device, device_id_type=MESH,
        )

    mine = 2 * c + xh
    my_rows = pl.ds(pl.multiple_of(g * 16, 16), 16)
    loads[0].wait()
    for xh_ in range(2):
        for z_ in range(NZ):
            for c_ in range(2):
                first = (xh_ * 16 + z_ * 2 + c_) * COL
                tp[2 * c_ + xh_, :, z_ * COL : (z_ + 1) * COL] = tv[:, first : first + COL]
    t1[mine] = tp[mine]
    my_cols = pl.ds(pl.multiple_of(z * COL, COL), COL)
    for s in range(4):
        t2[4 * z + s, my_rows, :] = tp[s, my_rows, my_cols]
    loads[2].wait()
    loads[3].wait()
    for u in range(NU):
        cols = slice(u * UNIT, (u + 1) * UNIT)
        wide = gv[:, cols].astype(F32)
        hg[z, u] = (wide * jax.nn.sigmoid(wide) * uv[:, cols].astype(F32)).astype(BF16)
    loads[1].wait()
    pl.semaphore_wait(barrier, len(partners))

    def origin(way, s):
        return (z - s + 8) % 8 if way == 0 else (z + s) % 8

    def w_copy(way, s, p, org):
        first, rows = W_GROUPS[p][way]
        ref = wg.at[org, pl.ds(first, rows)]
        return remote(ref, ref, ws.at[way, s, p], wr.at[way, s, p], (ahead, behind)[way])

    def w_send(s, p):
        for way in range(2):
            w_copy(way, s, p, origin(way, s)).start()

    def w_arrived(s, p):
        for way in range(2):
            w_copy(way, s, p, origin(way, s + 1)).wait_recv()

    def h_copy(way, s, p, org):
        first, units, _ = H_GROUPS[p]
        ref = hg.at[org, pl.ds(first, units), pl.ds(way * 64, 64), :]
        return remote(ref, ref, hs.at[way, s, p], hr.at[way, s, p], (ahead, behind)[way])

    def h_send(s, p):
        for way in range(2):
            h_copy(way, s, p, origin(way, s)).start()

    def h_arrived(s, p):
        for way in range(2):
            h_copy(way, s, p, origin(way, s + 1)).wait_recv()

    def h_tick(tick):
        for p, (_, _, begin) in enumerate(H_GROUPS):
            s = tick - begin
            if 1 <= s <= STEPS:
                h_arrived(s - 1, p)
            if 0 <= s < STEPS:
                h_send(s, p)

    t1_to = ((core, 2 * (1 - c) + xh), (xnb[0], 2 * c + 1 - xh), (xnb[1], 2 * (1 - c) + 1 - xh))

    def t1_copy(j, slot):
        return remote(tp.at[t1_to[j][1]], t1.at[slot], t1s.at[j], t1r.at[j], t1_to[j][0])

    def t2_across(k, at):
        cols = pl.ds(pl.multiple_of((z + k) % 8 * COL, COL), COL)
        return remote(
            tp.at[:, my_rows, cols], t2.at[pl.ds(4 * at, 4), my_rows, :],
            t2as.at[k], t2ar.at[k], z_at(k),
        )

    def t2_among(k, owner):
        rows = pl.ds(pl.multiple_of(owner * 16, 16), 16)
        ref = t2.at[:, rows, :]
        return remote(ref, ref, t2gs.at[k], t2gr.at[k], g_at(k))

    for p in range(len(W_GROUPS)):
        w_send(0, p)
    for j in range(3):
        t1_copy(j, mine).start()
    for k in range(1, 8):
        t2_across(k, z).start()

    loads[4].wait()
    acc = jnp.zeros((TOK, 128), F32)
    for i in range(4):
        cols = pl.ds(pl.multiple_of(g * 512 + i * 128, 128), 128)
        acc += rv[:, i * 128 : (i + 1) * 128].astype(F32) * tv[:, cols].astype(F32)

    for s in range(1, STEPS):
        for p in range(len(W_GROUPS)):
            w_arrived(s - 1, p)
            w_send(s, p)
        if s == 2:
            for k in range(1, 8):
                t2_across(k, (z - k + 8) % 8).wait_recv()
            for k in range(1, 8):
                t2_among(k, g).start()
        if s == 4:
            for k in range(1, 8):
                t2_among(k, (g - k + 8) % 8).wait_recv()

            def turn(i, carry):
                at = pl.ds(pl.multiple_of(i * TOK, TOK), TOK)
                for c_ in range(2):
                    for xh_ in range(2):
                        block = t2[4 * i + 2 * c_ + xh_].astype(F32)
                        t2t[c_, xh_ * COL : (xh_ + 1) * COL, at] = block.T.astype(BF16)
                return carry

            lax.fori_loop(0, NZ, turn, 0)
        if s == 5:
            for j in range(3):
                t1_copy(j, t1_to[j][1]).wait_recv()

    nt = (((1,), (1,)), ((), ()))

    def core_copy(u):
        return remote(cs.at[u], cr.at[u], css.at[u], crs.at[u], core)

    def x_copy(u):
        return remote(xs.at[u], xr.at[u], xss.at[u], xrs.at[u], xopp)

    def product(u):
        rows = pl.ds(u * UNIT, UNIT)
        block = jnp.concatenate([wg[i, rows, :] for i in range(NZ)], axis=1)
        for half, where in ((1 - c, None), (c, pm)):
            lhs = t1[pl.ds(2 * half, 2)].reshape(2 * TOK, NZ * COL)
            out = lax.dot_general(lhs, block, nt, preferred_element_type=F32)
            if where is None:
                cs[u] = out.astype(BF16).reshape(2, TOK, UNIT)
                core_copy(u).start()
            else:
                where[u] = out.reshape(2, TOK, UNIT)

    def across_x(u):
        core_copy(u).wait_recv()
        xs[u] = (pm[u, 1 - xh] + cr[u, 1 - xh].astype(F32)).astype(BF16)
        x_copy(u).start()

    def back_of(u, acc):
        x_copy(u).wait_recv()
        back = pm[u, xh] + cr[u, xh].astype(F32) + xr[u].astype(F32)
        bk[u] = back
        weighted = back * hg[z, u].astype(F32)
        return acc + weighted[:, :128] + weighted[:, 128:]

    tick = 0
    h_tick(tick)
    tick += 1
    w_arrived(STEPS - 1, 0)
    for u in range(4):
        product(u)
    h_tick(tick)
    tick += 1
    w_arrived(STEPS - 1, 1)
    for u in range(4, NU):
        across_x(u - 4)
        product(u)
    across_x(3)
    h_tick(tick)
    tick += 1
    for u in range(4, NU):
        across_x(u)
    h_tick(tick)
    tick += 1
    for u in range(NU):
        acc = back_of(u, acc)

    lane = lax.broadcasted_iota(jnp.int32, (1, TOK), 1)
    mask_row = mask[...].astype(F32)
    scores = jnp.sum(acc.T, axis=0, keepdims=True) * mask_row
    first_sum = jnp.sum(jnp.where(lane < L, scores, 0.0), axis=1, keepdims=True)
    second_sum = jnp.sum(jnp.where(lane < L, 0.0, scores), axis=1, keepdims=True)
    row = lax.broadcasted_iota(jnp.int32, (8, 128), 0)
    sb[g] = jnp.where(row == 0, first_sum, second_sum)

    def sum_copy(k, owner):
        return remote(sb.at[owner], sb.at[owner], sbs.at[k], sbr.at[k], g_at(k))

    def factor_copy(k, owner):
        return remote(fg.at[owner], fg.at[owner], fgs.at[k], fgr.at[k], z_at(k))

    for k in range(1, 8):
        sum_copy(k, g).start()
    h_tick(tick)
    tick += 1
    for k in range(1, 8):
        sum_copy(k, (g - k + 8) % 8).wait_recv()
    total = sb[0]
    for i in range(1, 8):
        total = total + sb[i]
    count0 = cnt[0].astype(F32)
    count1 = cnt[1].astype(F32)
    reward0 = beta_coef * total[0:1, :] / count0
    reward1 = beta_coef * total[1:2, :] / count1
    margin = reward0 - reward1 - gamma_margin
    pair = jnp.maximum(-margin, 0.0) + jnp.log1p(jnp.exp(-jnp.abs(margin)))
    loss[0] = pair[0, 0]
    weight = jax.nn.sigmoid(-margin) * loss_scale * beta_coef
    factor = jnp.where(lane < L, -weight / count0, weight / count1) * mask_row
    fg[z] = jnp.broadcast_to(factor, (8, 128))
    for k in range(1, 8):
        factor_copy(k, z).start()
    h_tick(tick)
    tick += 1

    by_row = jnp.broadcast_to(factor, (TOK, 128)).T
    by_row = jnp.concatenate([by_row, by_row], axis=1)
    for u in range(NU):
        cols = slice(u * UNIT, (u + 1) * UNIT)
        wide = gv[:, cols].astype(F32)
        sig = jax.nn.sigmoid(wide)
        grad = by_row * bk[u]
        swish = wide * sig
        ggv[:, cols] = (grad * uv[:, cols].astype(F32) * (sig + swish * (1.0 - sig))).astype(BF16)
        guv[:, cols] = (grad * swish).astype(BF16)
    out_copies = [
        pltpu.make_async_copy(ggv, gg, out_sem.at[0]),
        pltpu.make_async_copy(guv, gu, out_sem.at[1]),
    ]
    for copy in out_copies:
        copy.start()
    h_tick(tick)
    tick += 1
    for k in range(1, 8):
        factor_copy(k, (z - k + 8) % 8).wait_recv()

    def scale(i, carry):
        at = pl.ds(pl.multiple_of(i * TOK, TOK), TOK)
        by_lane = fg[i][0:1, :]
        for c_ in range(2):
            t2s[c_, :, at] = (t2t[c_, :, at].astype(F32) * by_lane).astype(BF16)
        return carry

    lax.fori_loop(0, NZ, scale, 0)

    nn = (((1,), (0,)), ((), ()))

    def core_copy2(u):
        return remote(cs2.at[u], cr2.at[u], css2.at[u], crs2.at[u], core)

    def x_copy2(u):
        return remote(xs2.at[u], xr2.at[u], xss2.at[u], xrs2.at[u], xopp)

    def product2(u):
        rhs = hg[:, u].reshape(NZ * TOK, UNIT)
        out = lax.dot_general(t2s[1 - c], rhs, nn, preferred_element_type=F32)
        cs2[u] = out.astype(BF16).reshape(2, COL, UNIT)
        core_copy2(u).start()
        out = lax.dot_general(t2s[c], rhs, nn, preferred_element_type=F32)
        dm[u] = out.reshape(2, COL, UNIT)

    def across_x2(u):
        core_copy2(u).wait_recv()
        xs2[u] = (dm[u, 1 - xh] + cr2[u, 1 - xh].astype(F32)).astype(BF16)
        x_copy2(u).start()

    def write(u):
        x_copy2(u).wait_recv()
        rows = pl.ds(u * UNIT, UNIT)
        gdv[rows, :] = (dm[u, xh] + cr2[u, xh].astype(F32) + xr2[u].astype(F32)).T
        copy = pltpu.make_async_copy(gdv.at[rows], gd.at[rows], out_sem.at[2 + u])
        copy.start()
        out_copies.append(copy)

    last_tick = STEPS + H_GROUPS[-1][2]
    ready = 0
    done = []
    while tick <= last_tick:
        h_tick(tick)
        tick += 1
        while ready < len(H_GROUPS) and tick > STEPS + H_GROUPS[ready][2]:
            first, units, _ = H_GROUPS[ready]
            for u in range(first, first + units):
                product2(u)
            for u in range(first, first + units):
                across_x2(u)
                done.append(u)
            ready += 1
    for u in done:
        write(u)

    for s in range(STEPS):
        for way in range(2):
            for p in range(len(W_GROUPS)):
                w_copy(way, s, p, origin(way, s)).wait_send()
            for p in range(len(H_GROUPS)):
                h_copy(way, s, p, origin(way, s)).wait_send()
    for j in range(3):
        t1_copy(j, mine).wait_send()
    for k in range(1, 8):
        t2_across(k, z).wait_send()
        t2_among(k, g).wait_send()
        sum_copy(k, g).wait_send()
        factor_copy(k, z).wait_send()
    for u in range(NU):
        core_copy(u).wait_send()
        x_copy(u).wait_send()
        core_copy2(u).wait_send()
        x_copy2(u).wait_send()
    for copy in out_copies:
        copy.wait()


def on_device(gate_pre, up_pre, down_weight, residual, target_rows, loss_mask, response_count):
    any_space = pl.BlockSpec(memory_space=pl.ANY)
    smem = pl.BlockSpec(memory_space=pltpu.SMEM)
    vmem = pl.BlockSpec(memory_space=pltpu.VMEM)
    sem = pltpu.SemaphoreType.DMA
    scratch = [
        pltpu.VMEM((TOK, HID), BF16),
        pltpu.VMEM((TOK, HID), BF16),
        pltpu.VMEM((TOK, 512), BF16),
        pltpu.VMEM((TOK, D), BF16),
        pltpu.VMEM((4, TOK, NZ * COL), BF16),
        pltpu.VMEM((4, TOK, NZ * COL), BF16),
        pltpu.VMEM((4 * NZ, TOK, COL), BF16),
        pltpu.VMEM((2, 2 * COL, NZ * TOK), BF16),
        pltpu.VMEM((2, 2 * COL, NZ * TOK), BF16),
        pltpu.VMEM((NZ, HID, COL), BF16),
        pltpu.VMEM((NZ, NU, TOK, UNIT), BF16),
        pltpu.VMEM((NU, 2, TOK, UNIT), F32),
        pltpu.VMEM((NU, 2, TOK, UNIT), BF16),
        pltpu.VMEM((NU, 2, TOK, UNIT), BF16),
        pltpu.VMEM((NU, TOK, UNIT), BF16),
        pltpu.VMEM((NU, TOK, UNIT), BF16),
        pltpu.VMEM((NU, TOK, UNIT), F32),
        pltpu.VMEM((NU, 2, COL, UNIT), F32),
        pltpu.VMEM((NU, 2, COL, UNIT), BF16),
        pltpu.VMEM((NU, 2, COL, UNIT), BF16),
        pltpu.VMEM((NU, COL, UNIT), BF16),
        pltpu.VMEM((NU, COL, UNIT), BF16),
        pltpu.VMEM((TOK, HID), BF16),
        pltpu.VMEM((TOK, HID), BF16),
        pltpu.VMEM((HID, COL), F32),
        pltpu.VMEM((8, 8, 128), F32),
        pltpu.VMEM((8, 8, 128), F32),
        sem((5,)),
        sem((2 + NU,)),
        sem((2, STEPS, len(W_GROUPS))),
        sem((2, STEPS, len(W_GROUPS))),
        sem((2, STEPS, len(H_GROUPS))),
        sem((2, STEPS, len(H_GROUPS))),
        sem((3,)),
        sem((3,)),
        *[sem((8,)) for _ in range(4)],
        *[sem((NU,)) for _ in range(8)],
        *[sem((8,)) for _ in range(4)],
    ]
    macs = 2 * 4 * TOK * NZ * COL * HID
    loss, grad_gate, grad_up, grad_down = pl.pallas_call(
        kernel,
        out_shape=(
            jax.ShapeDtypeStruct((1,), F32),
            jax.ShapeDtypeStruct(gate_pre.shape, BF16),
            jax.ShapeDtypeStruct(gate_pre.shape, BF16),
            jax.ShapeDtypeStruct(down_weight.shape, F32),
        ),
        in_specs=[any_space] * 5 + [vmem, smem],
        out_specs=(smem, any_space, any_space, any_space),
        scratch_shapes=scratch,
        compiler_params=pltpu.CompilerParams(
            collective_id=0, has_side_effects=True, vmem_limit_bytes=56 << 20
        ),
        cost_estimate=pl.CostEstimate(flops=2 * macs, bytes_accessed=6 << 20, transcendentals=0),
    )(
        gate_pre, up_pre, down_weight, residual, target_rows,
        loss_mask.reshape(1, TOK), response_count,
    )
    return loss, grad_gate, grad_up, grad_down


def solution(mesh):
    placed = (
        P("fsdp", "tensor"),
        P("fsdp", "tensor"),
        P("tensor", "fsdp"),
        P("fsdp", None),
        P("fsdp", None),
        P("fsdp"),
        P("fsdp"),
    )
    return jax.shard_map(
        on_device,
        mesh=mesh,
        in_specs=placed,
        out_specs=(P("fsdp"), P("fsdp", "tensor"), P("fsdp", "tensor"), P("tensor", "fsdp")),
        check_vma=False,
    )
```

```python
import functools

import jax
import jax.numpy as jnp
from jax import lax
from jax.experimental import pallas as pl
from jax.experimental.pallas import tpu as pltpu
from jax.sharding import PartitionSpec as P

MESH = pl.DeviceIdType.MESH
F32 = jnp.float32
BF16 = jnp.bfloat16

beta_coef = 2.0
gamma_margin = 1.0
loss_scale = 1024.0

L = 64
NZ = 8
TOK = 128
COL = 128
UNIT = 256
NU = 7
HID = UNIT * NU
D = 4096

W_GROUPS = ((0, 4, 0), (4, 3, 0))
H_GROUPS = ((0, 2, 4), (2, 2, 5), (4, 2, 6), (6, 1, 7))
STEPS = NZ - 1


AFTER = {
    (2, "W", 1): [("pass",), ("hid",)],
    (4, "W", 1): [("turn",)],
    (6, "W", 1): [("t1",), ("hids",)],
    (7, "W", 0): [("P", 0), ("P", 1), ("P", 2), ("P", 3)],
    (7, "W", 1): [("P", 4), ("P", 5), ("P", 6), ("rows",)],
    (7, "H", 3): [("flush",)],
    (8, "H", 0): [("sum",)],
    (9, "H", 0): [("factor",)],
    (9, "H", 3): [("PX",)],
    (10, "H", 3): [("scale",)],
    (11, "H", 3): [("D", 0), ("D", 1), ("PB",), ("DX", 0), ("DX", 1)],
    (12, "H", 3): [("D", 2), ("D", 3), ("grad", 0, 7), ("DX", 2), ("DX", 3)],
    (13, "H", 3): [("D", 4), ("D", 5), ("DO", 0), ("DO", 1), ("DX", 4), ("DX", 5), ("rest",)],
    (14, "H", 3): [("D", 6), ("DO", 2), ("DX", 6), ("DO", 3), ("DO", 4), ("DO", 5), ("DO", 6)],
}


def make_schedule():
    order = []
    for tick in range(15):
        for kind, groups in (("W", W_GROUPS), ("H", H_GROUPS)):
            for p, (_, _, begin) in enumerate(groups):
                if begin <= tick <= begin + STEPS and (tick > 0 or kind != "W"):
                    order.append((kind, p, tick))
                order += AFTER.get((tick, kind, p), [])
    return order


SCHEDULE = make_schedule()


def kernel(
    gate, up, w, resid, tgt, mask, cnt, loss, gg, gu, gd,
    gv, uv, rv, tv, tp, t1, t2, t2t, t2s, wg, hg, pm, cs, cr, xs, xr, bk,
    dm, cs2, cr2, xs2, xr2, ggv, guv, gdv, sb, fg, score_acc, ha, rb, rc, maskv, cntv, lossv,
    ld_sem, out_sem, ws, wr, hs, hr, t1s, t1r, t2as, t2ar, t2gs, t2gr,
    css, crs, xss, xrs, css2, crs2, xss2, xrs2, sbs, sbr, fgs, fgr, has, har, rbs, rbr,
):
    f = lax.axis_index("fsdp")
    g = lax.axis_index("tensor")
    xh, z, c = f // 16, (f // 2) % 8, f % 2
    xl, y = g // 4, g % 4

    def place(xh_, z_, c_, xl_=xl, y_=y):
        return (xh_ * 16 + z_ * 2 + c_, xl_ * 4 + y_)

    def z_at(k):
        return (f // 16 * 16 + (z + k) % 8 * 2 + c, g)

    def g_at(k):
        return (f, (g + k) % 8)

    core = place(xh, z, 1 - c)
    xopp = place(1 - xh, z, c)
    xopp2 = place(1 - xh, z, 1 - c)
    xnb = (place(1 - xh, z, c, 1 - xl), place(1 - xh, z, 1 - c, 1 - xl))
    ahead, behind = z_at(1), z_at(7)

    barrier = pltpu.get_barrier_semaphore()
    partners = [z_at(k) for k in range(1, 8)] + [g_at(k) for k in range(1, 8)]
    partners += [core, xopp, xopp2, *xnb]
    for partner in partners:
        pl.semaphore_signal(barrier, inc=1, device_id=partner, device_id_type=MESH)

    loads = [
        pltpu.make_async_copy(tgt, tv, ld_sem.at[0]),
        pltpu.make_async_copy(w, wg.at[z], ld_sem.at[1]),
        pltpu.make_async_copy(gate, gv, ld_sem.at[2]),
        pltpu.make_async_copy(up, uv, ld_sem.at[3]),
        pltpu.make_async_copy(
            resid.at[:, pl.ds(pl.multiple_of(g * 512, 512), 512)], rv, ld_sem.at[4]
        ),
        pltpu.make_async_copy(mask, maskv, ld_sem.at[5]),
        pltpu.make_async_copy(cnt, cntv, ld_sem.at[6]),
    ]
    for load in loads:
        load.start()

    out_copies = []

    def remote(src, dst, sems, at, device):
        return pltpu.make_async_remote_copy(
            src_ref=src, dst_ref=dst, send_sem=sems[0].at[at[0]], recv_sem=sems[1].at[at[1]],
            device_id=device, device_id_type=MESH,
        )

    def send(copy):
        copy.start()

    def take(ref, sem):
        pltpu.make_async_copy(ref, ref, sem).wait()

    loads[1].wait()
    pl.semaphore_wait(barrier, len(partners))

    def origin(way, s):
        return (z - s + 8) % 8 if way == 0 else (z + s) % 8

    def w_copy(way, s, p, org):
        first, units, _ = W_GROUPS[p]
        rows = units * UNIT // 2
        ref = wg.at[org, pl.ds(first * UNIT + way * rows, rows)]
        return remote(ref, ref, (ws, wr), ((way, p), (way, s, p)), (ahead, behind)[way])

    def h_copy(way, s, p, org):
        first, units, _ = H_GROUPS[p]
        ref = hg.at[org, pl.ds(first, units), pl.ds(way * 64, 64), :]
        return remote(ref, ref, (hs, hr), ((way, p), (way, s, p)), (ahead, behind)[way])

    def w_step(p, tick):
        s = tick - W_GROUPS[p][2]
        for way in range(2):
            if s >= 1:
                w_copy(way, s - 1, p, origin(way, s)).wait_recv()
                w_copy(way, s - 1, p, origin(way, s - 1)).wait_send()
            if s < STEPS:
                w_copy(way, s, p, origin(way, s)).start()

    def h_step(p, tick):
        s = tick - H_GROUPS[p][2]
        for way in range(2):
            if s >= 1:
                h_copy(way, s - 1, p, origin(way, s)).wait_recv()
                h_copy(way, s - 1, p, origin(way, s - 1)).wait_send()
            if s < STEPS:
                h_copy(way, s, p, origin(way, s)).start()

    for p in range(len(W_GROUPS)):
        w_step(p, 0)

    mine = 2 * c + xh
    my_rows = pl.ds(pl.multiple_of(g * 16, 16), 16)
    loads[0].wait()
    for xh_ in range(2):
        for z_ in range(NZ):
            for c_ in range(2):
                first = (xh_ * 16 + z_ * 2 + c_) * COL
                tp[2 * c_ + xh_, :, z_ * COL : (z_ + 1) * COL] = tv[:, first : first + COL]
    t1[mine] = tp[mine]
    my_cols = pl.ds(pl.multiple_of(z * COL, COL), COL)
    for s in range(4):
        t2[4 * z + s, my_rows, :] = tp[s, my_rows, my_cols]

    t1_to = ((core, 2 * (1 - c) + xh), (xnb[0], 2 * c + 1 - xh), (xnb[1], 2 * (1 - c) + 1 - xh))

    def t1_copy(j, slot):
        return remote(tp.at[t1_to[j][1]], t1.at[slot], (t1s, t1r), (0, 0), t1_to[j][0])

    def t2_across(k, at):
        cols = pl.ds(pl.multiple_of((z + k) % 8 * COL, COL), COL)
        return remote(
            tp.at[:, my_rows, cols], t2.at[pl.ds(4 * at, 4), my_rows, :],
            (t2as, t2ar), (0, 0), z_at(k),
        )

    def t2_among(k, owner):
        rows = pl.ds(pl.multiple_of(owner * 16, 16), 16)
        ref = t2.at[:, rows, :]
        return remote(ref, ref, (t2gs, t2gr), (0, 0), g_at(k))

    for j in range(3):
        send(t1_copy(j, mine))
    for k in range(1, 8):
        send(t2_across(k, z))

    ha_to = (xopp, core, core)

    def ha_copy(j, slot):
        ref = ha.at[slot]
        return remote(ref, ref, (has, har), (0, j), ha_to[j])

    loads[2].wait()
    loads[3].wait()
    for u in range(NU):
        cols = slice(u * UNIT, (u + 1) * UNIT)
        wide = gv[:, cols].astype(F32)
        hidden = (wide * jax.nn.sigmoid(wide) * uv[:, cols].astype(F32)).astype(BF16)
        hg[z, u] = hidden
        ha[mine, u] = hidden
    send(ha_copy(0, mine))
    send(ha_copy(1, mine))

    loads[4].wait()
    loads[5].wait()
    loads[6].wait()
    acc = jnp.zeros((TOK, 128), F32)
    for i in range(4):
        cols = pl.ds(pl.multiple_of(g * 512 + i * 128, 128), 128)
        acc += rv[:, i * 128 : (i + 1) * 128].astype(F32) * tv[:, cols].astype(F32)
    score_acc[...] = jnp.zeros_like(score_acc)
    score_acc[mine] = acc

    def hidden_pass_on():
        ha_copy(0, 2 * c + 1 - xh).wait_recv()
        send(ha_copy(2, 2 * c + 1 - xh))

    def hidden_here():
        ha_copy(1, 2 * (1 - c) + xh).wait_recv()
        ha_copy(2, 2 * (1 - c) + 1 - xh).wait_recv()

    def t2_pass_on():
        take(t2.at[pl.ds(0, 28), pl.ds(0, 16), :], t2ar.at[0])
        for k in range(1, 8):
            send(t2_among(k, g))

    def t2_turn():
        take(t2.at[:, pl.ds(0, 112), :], t2gr.at[0])

        def turn(i, carry):
            at = pl.ds(pl.multiple_of(i * TOK, TOK), TOK)
            for c_ in range(2):
                for xh_ in range(2):
                    block = t2[4 * i + 2 * c_ + xh_].astype(F32)
                    t2t[c_, xh_ * COL : (xh_ + 1) * COL, at] = block.T.astype(BF16)
            return carry

        lax.fori_loop(0, NZ, turn, 0)

    def t1_wait():
        take(t1.at[pl.ds(0, 3)], t1r.at[0])

    nt = (((1,), (1,)), ((), ()))

    def core_copy(u):
        return remote(cs.at[u], cr.at[u], (css, crs), (0, 0), core)

    def x_copy(u):
        return remote(xs.at[u], xr.at[u], (xss, xrs), (0, 0), xopp)

    def product(u):
        rows = pl.ds(u * UNIT, UNIT)
        block = jnp.concatenate([wg[i, rows, :] for i in range(NZ)], axis=1)
        for half, where in ((1 - c, None), (c, pm)):
            pair = pl.ds(2 * half, 2)
            lhs = t1[pair].reshape(2 * TOK, NZ * COL)
            out = lax.dot_general(lhs, block, nt, preferred_element_type=F32)
            out = out.reshape(2, TOK, UNIT)
            weighted = out * ha[pair, u].astype(F32)
            score_acc[pair] += weighted[:, :, :128] + weighted[:, :, 128:]
            if where is None:
                cs[u] = out.astype(BF16)
                send(core_copy(u))
            else:
                where[u] = out

    def across_x():
        take(cr, crs.at[0])
        for u in range(NU):
            xs[u] = (pm[u, 1 - xh] + cr[u, 1 - xh].astype(F32)).astype(BF16)
            send(x_copy(u))

    def back_of():
        take(xr, xrs.at[0])
        for u in range(NU):
            bk[u] = pm[u, xh] + cr[u, xh].astype(F32) + xr[u].astype(F32)

    lane = lax.broadcasted_iota(jnp.int32, (1, TOK), 1)

    def mask_row():
        return maskv[...].astype(F32)

    def sum_copy(k, owner):
        return remote(sb.at[owner], sb.at[owner], (sbs, sbr), (0, 0), g_at(k))

    def factor_copy(k, owner):
        return remote(fg.at[owner], fg.at[owner], (fgs, fgr), (0, 0), z_at(k))

    row_to = (
        (2 * (1 - c) + xh, core), (2 * c + 1 - xh, xopp), (2 * (1 - c) + 1 - xh, xopp2)
    )

    def row_copy(j):
        return remote(rb.at[j], rc.at[j], (rbs, rbr), (0, 0), row_to[j][1])

    def score_rows():
        for j in range(3):
            row = jnp.sum(score_acc[row_to[j][0]].T, axis=0, keepdims=True)
            rb[j] = jnp.broadcast_to(row, (8, TOK))
            send(row_copy(j))

    def sums():
        scores = jnp.sum(score_acc[mine].T, axis=0, keepdims=True)
        take(rc, rbr.at[0])
        scores = (scores + rc[0, 0:1, :] + rc[1, 0:1, :] + rc[2, 0:1, :]) * mask_row()
        first_sum = jnp.sum(jnp.where(lane < L, scores, 0.0), axis=1, keepdims=True)
        second_sum = jnp.sum(jnp.where(lane < L, 0.0, scores), axis=1, keepdims=True)
        row = lax.broadcasted_iota(jnp.int32, (8, 128), 0)
        sb[g] = jnp.where(row == 0, first_sum, second_sum)
        for k in range(1, 8):
            send(sum_copy(k, g))

    def factors():
        take(sb.at[pl.ds(0, 7)], sbr.at[0])
        total = sb[0]
        for i in range(1, 8):
            total = total + sb[i]
        count0 = cntv[0].astype(F32)
        count1 = cntv[1].astype(F32)
        reward0 = beta_coef * total[0:1, :] / count0
        reward1 = beta_coef * total[1:2, :] / count1
        margin = reward0 - reward1 - gamma_margin
        weight = jax.nn.sigmoid(-margin) * loss_scale * beta_coef
        factor = jnp.where(lane < L, -weight / count0, weight / count1) * mask_row()
        fg[z] = jnp.broadcast_to(factor, (8, 128))
        for k in range(1, 8):
            send(factor_copy(k, z))
        pair = jnp.maximum(-margin, 0.0) + jnp.log1p(jnp.exp(-jnp.abs(margin)))
        lossv[0] = pair[0, 0]
        out_copies.append(pltpu.make_async_copy(lossv, loss, out_sem.at[3]))
        out_copies[-1].start()

    def grads(first, units):
        by_row = jnp.broadcast_to(fg[z][0:1, :], (TOK, 128)).T
        by_row = jnp.concatenate([by_row, by_row], axis=1)
        for u in range(first, first + units):
            cols = slice(u * UNIT, (u + 1) * UNIT)
            wide = gv[:, cols].astype(F32)
            sig = jax.nn.sigmoid(wide)
            grad = by_row * bk[u]
            swish = wide * sig
            slope = sig + swish * (1.0 - sig)
            ggv[:, cols] = (grad * uv[:, cols].astype(F32) * slope).astype(BF16)
            guv[:, cols] = (grad * swish).astype(BF16)
        if first + units == NU:
            out_copies.append(pltpu.make_async_copy(ggv, gg, out_sem.at[0]))
            out_copies.append(pltpu.make_async_copy(guv, gu, out_sem.at[1]))
            for copy in out_copies[-2:]:
                copy.start()

    def scaled():
        take(fg.at[pl.ds(0, 7)], fgr.at[0])

        def scale(i, carry):
            at = pl.ds(pl.multiple_of(i * TOK, TOK), TOK)
            by_lane = fg[i][0:1, :]
            for c_ in range(2):
                t2s[c_, :, at] = (t2t[c_, :, at].astype(F32) * by_lane).astype(BF16)
            return carry

        lax.fori_loop(0, NZ, scale, 0)

    nn = (((1,), (0,)), ((), ()))

    def core_copy2(u):
        return remote(cs2.at[u], cr2.at[u], (css2, crs2), (0, u), core)

    def x_copy2(u):
        return remote(xs2.at[u], xr2.at[u], (xss2, xrs2), (0, u), xopp)

    def product2(u):
        rhs = hg[:, u].reshape(NZ * TOK, UNIT)
        out = lax.dot_general(t2s[1 - c], rhs, nn, preferred_element_type=F32)
        cs2[u] = out.astype(BF16).reshape(2, COL, UNIT)
        send(core_copy2(u))
        out = lax.dot_general(t2s[c], rhs, nn, preferred_element_type=F32)
        dm[u] = out.reshape(2, COL, UNIT)

    def across_x2(u):
        core_copy2(u).wait_recv()
        xs2[u] = (dm[u, 1 - xh] + cr2[u, 1 - xh].astype(F32)).astype(BF16)
        send(x_copy2(u))

    def write(u):
        x_copy2(u).wait_recv()
        rows = pl.ds(u * UNIT, UNIT)
        gdv[rows, :] = (dm[u, xh] + cr2[u, xh].astype(F32) + xr2[u].astype(F32)).T
        copy = pltpu.make_async_copy(gdv.at[rows], gd.at[rows], out_sem.at[2])
        copy.start()

    def flush():
        take(t1.at[pl.ds(0, 3)], t1s.at[0])
        take(t2.at[pl.ds(0, 28), pl.ds(0, 16), :], t2as.at[0])
        take(t2.at[:, pl.ds(0, 112), :], t2gs.at[0])
        take(ha.at[pl.ds(0, 3)], has.at[0])

    def flush_rest():
        take(rb, rbs.at[0])
        take(sb.at[pl.ds(0, 7)], sbs.at[0])
        take(fg.at[pl.ds(0, 7)], fgs.at[0])
        take(cs, css.at[0])
        take(xs, xss.at[0])

    tasks = {
        "W": w_step, "H": h_step, "pass": t2_pass_on, "turn": t2_turn, "t1": t1_wait,
        "P": product, "PX": across_x, "PB": back_of, "sum": sums, "factor": factors, "rows": score_rows, "hid": hidden_pass_on, "hids": hidden_here,
        "grad": grads, "scale": scaled, "D": product2, "DX": across_x2, "DO": write,
        "flush": flush, "rest": flush_rest,
    }
    for name, *given in SCHEDULE:
        tasks[name](*given)

    take(cs2, css2.at[0])
    take(xs2, xss2.at[0])
    take(gdv, out_sem.at[2])
    for copy in out_copies:
        copy.wait()


def hand_over(*refs):
    sems = refs[-1]
    fetch = [pltpu.make_async_copy(refs[i], refs[6 + i], sems.at[0, i]) for i in range(3)]
    store = [pltpu.make_async_copy(refs[6 + i], refs[3 + i], sems.at[1, i]) for i in range(3)]
    for copy in fetch:
        copy.start()
    for i in range(3):
        fetch[i].wait()
        store[i].start()
    for copy in store:
        copy.wait()


def on_device(gate_pre, up_pre, down_weight, residual, target_rows, loss_mask, response_count):
    any_space = pl.BlockSpec(memory_space=pl.ANY)
    sem = pltpu.SemaphoreType.DMA
    scratch = [
        pltpu.VMEM((TOK, HID), BF16),
        pltpu.VMEM((TOK, HID), BF16),
        pltpu.VMEM((TOK, 512), BF16),
        pltpu.VMEM((TOK, D), BF16),
        pltpu.VMEM((4, TOK, NZ * COL), BF16),
        pltpu.VMEM((4, TOK, NZ * COL), BF16),
        pltpu.VMEM((4 * NZ, TOK, COL), BF16),
        pltpu.VMEM((2, 2 * COL, NZ * TOK), BF16),
        pltpu.VMEM((2, 2 * COL, NZ * TOK), BF16),
        pltpu.VMEM((NZ, HID, COL), BF16),
        pltpu.VMEM((NZ, NU, TOK, UNIT), BF16),
        pltpu.VMEM((NU, 2, TOK, UNIT), F32),
        pltpu.VMEM((NU, 2, TOK, UNIT), BF16),
        pltpu.VMEM((NU, 2, TOK, UNIT), BF16),
        pltpu.VMEM((NU, TOK, UNIT), BF16),
        pltpu.VMEM((NU, TOK, UNIT), BF16),
        pltpu.VMEM((NU, TOK, UNIT), F32),
        pltpu.VMEM((NU, 2, COL, UNIT), F32),
        pltpu.VMEM((NU, 2, COL, UNIT), BF16),
        pltpu.VMEM((NU, 2, COL, UNIT), BF16),
        pltpu.VMEM((NU, COL, UNIT), BF16),
        pltpu.VMEM((NU, COL, UNIT), BF16),
        pltpu.VMEM((TOK, HID), BF16),
        pltpu.VMEM((TOK, HID), BF16),
        pltpu.VMEM((HID, COL), F32),
        pltpu.VMEM((8, 8, 128), F32),
        pltpu.VMEM((8, 8, 128), F32),
        pltpu.VMEM((4, TOK, 128), F32),
        pltpu.VMEM((4, NU, TOK, UNIT), BF16),
        pltpu.VMEM((3, 8, TOK), F32),
        pltpu.VMEM((3, 8, TOK), F32),
        pltpu.VMEM((1, TOK), jnp.int32),
        pltpu.SMEM((2,), jnp.int32),
        pltpu.SMEM((1,), F32),
        sem((7,)),
        sem((4,)),
        sem((2, len(W_GROUPS))),
        sem((2, STEPS, len(W_GROUPS))),
        sem((2, len(H_GROUPS))),
        sem((2, STEPS, len(H_GROUPS))),
        *[sem((1,)) for _ in range(6)],
        *[sem((1,)) for _ in range(5)],
        sem((NU,)),
        sem((1,)),
        sem((NU,)),
        *[sem((1,)) for _ in range(4)],
        sem((1,)),
        sem((3,)),
        *[sem((1,)) for _ in range(2)],
    ]
    macs = 2 * 4 * TOK * NZ * COL * HID
    loss, grad_gate, grad_up, grad_down = pl.pallas_call(
        kernel,
        out_shape=(
            jax.ShapeDtypeStruct((1,), F32),
            jax.ShapeDtypeStruct(gate_pre.shape, BF16),
            jax.ShapeDtypeStruct(gate_pre.shape, BF16),
            jax.ShapeDtypeStruct(down_weight.shape, F32),
        ),
        in_specs=[any_space] * 7,
        out_specs=(any_space,) * 4,
        scratch_shapes=scratch,
        compiler_params=pltpu.CompilerParams(
            collective_id=0, has_side_effects=True, vmem_limit_bytes=56 << 20
        ),
        cost_estimate=pl.CostEstimate(flops=2 * macs, bytes_accessed=6 << 20, transcendentals=0),
    )(
        gate_pre, up_pre, down_weight, residual, target_rows,
        loss_mask.reshape(1, TOK), response_count,
    )
    grad_gate, grad_up, grad_down = pl.pallas_call(
        hand_over,
        out_shape=tuple(jax.ShapeDtypeStruct(a.shape, a.dtype) for a in (grad_gate, grad_up, grad_down)),
        in_specs=[any_space] * 3,
        out_specs=(any_space,) * 3,
        scratch_shapes=[
            pltpu.VMEM(gate_pre.shape, BF16),
            pltpu.VMEM(gate_pre.shape, BF16),
            pltpu.VMEM(down_weight.shape, F32),
            sem((2, 3)),
        ],
    )(grad_gate, grad_up, grad_down)
    return loss, grad_gate, grad_up, grad_down


def solution(mesh):
    placed = (
        P("fsdp", "tensor"),
        P("fsdp", "tensor"),
        P("tensor", "fsdp"),
        P("fsdp", None),
        P("fsdp", None),
        P("fsdp"),
        P("fsdp"),
    )
    return jax.shard_map(
        on_device,
        mesh=mesh,
        in_specs=placed,
        out_specs=(P("fsdp"), P("fsdp", "tensor"), P("fsdp", "tensor"), P("tensor", "fsdp")),
        check_vma=False,
    )
```

```python
import functools

import jax
import jax.numpy as jnp
from jax import lax
from jax.experimental import pallas as pl
from jax.experimental.pallas import tpu as pltpu
from jax.sharding import PartitionSpec as P

MESH = pl.DeviceIdType.MESH
F32 = jnp.float32
BF16 = jnp.bfloat16

beta_coef = 2.0
gamma_margin = 1.0
loss_scale = 1024.0

L = 64
NZ = 8
TOK = 128
COL = 128
UNIT = 256
NU = 7
HID = UNIT * NU
D = 4096

W_GROUPS = ((0, 4, 0), (4, 3, 0))
H_GROUPS = ((0, 2, 4), (2, 2, 5), (4, 2, 6), (6, 1, 7))
STEPS = NZ - 1


EARLY = {
    (2, "W", 1): [("pass",), ("hid",)],
    (4, "W", 1): [("turn",)],
    (6, "W", 1): [("t1",), ("hids",)],
    (7, "W", 0): [("P", 0), ("P", 1), ("P", 2), ("P", 3)],
    (7, "W", 1): [("P", 4), ("P", 5), ("P", 6), ("rows",)],
    (8, "H", 0): [("sum",)],
    (9, "H", 0): [("factor",)],
}


def make_schedule():
    after = dict(EARLY)
    last = len(H_GROUPS) - 1
    ends = [begin + STEPS for _, _, begin in H_GROUPS]
    after[7, "H", last] = [("flush",)]
    after[8, "H", last] = [("PX",)]
    after[10, "H", last] = [("scale",), ("PB",), ("grad", 0, 7)]
    for p, (first, units, _) in enumerate(H_GROUPS):
        group = range(first, first + units)
        todo = after.setdefault((ends[p], "H", last), [])
        todo += [("D", u) for u in group]
        todo += [("rest",)] if p == last else []
        todo += [("DX", u) for u in group]
    todo += [("DO", u) for u in range(NU)]
    order = []
    for tick in range(ends[-1] + 1):
        for kind, groups in (("W", W_GROUPS), ("H", H_GROUPS)):
            for p, (_, _, begin) in enumerate(groups):
                if begin <= tick <= begin + STEPS and (tick > 0 or kind != "W"):
                    order.append((kind, p, tick))
                order += after.get((tick, kind, p), [])
    return order


SCHEDULE = make_schedule()


def kernel(
    gate, up, w, resid, tgt, mask, cnt, loss, gg, gu, gd,
    gv, uv, rv, tv, tp, t1, t2, t2t, t2s, wg, hg, pm, cs, cr, xs, xr, bk,
    dm, cs2, cr2, xs2, xr2, sb, fg, score_acc, ha, rb, rc, maskv, cntv, lossv,
    ld_sem, out_sem, ws, wr, hs, hr, t1s, t1r, t2as, t2ar, t2gs, t2gr,
    css, crs, xss, xrs, css2, crs2, xss2, xrs2, sbs, sbr, fgs, fgr, has, har, rbs, rbr,
):
    f = lax.axis_index("fsdp")
    g = lax.axis_index("tensor")
    xh, z, c = f // 16, (f // 2) % 8, f % 2
    xl, y = g // 4, g % 4

    def place(xh_, z_, c_, xl_=xl, y_=y):
        return (xh_ * 16 + z_ * 2 + c_, xl_ * 4 + y_)

    def z_at(k):
        return (f // 16 * 16 + (z + k) % 8 * 2 + c, g)

    def g_at(k):
        return (f, (g + k) % 8)

    core = place(xh, z, 1 - c)
    xopp = place(1 - xh, z, c)
    xopp2 = place(1 - xh, z, 1 - c)
    xnb = (place(1 - xh, z, c, 1 - xl), place(1 - xh, z, 1 - c, 1 - xl))
    ahead, behind = z_at(1), z_at(7)

    barrier = pltpu.get_barrier_semaphore()
    partners = [z_at(k) for k in range(1, 8)] + [g_at(k) for k in range(1, 8)]
    partners += [core, xopp, xopp2, *xnb]
    for partner in partners:
        pl.semaphore_signal(barrier, inc=1, device_id=partner, device_id_type=MESH)

    loads = [
        pltpu.make_async_copy(tgt, tv, ld_sem.at[0]),
        pltpu.make_async_copy(w, wg.at[z], ld_sem.at[1]),
        pltpu.make_async_copy(gate, gv, ld_sem.at[2]),
        pltpu.make_async_copy(up, uv, ld_sem.at[3]),
        pltpu.make_async_copy(
            resid.at[:, pl.ds(pl.multiple_of(g * 512, 512), 512)], rv, ld_sem.at[4]
        ),
        pltpu.make_async_copy(mask, maskv, ld_sem.at[5]),
        pltpu.make_async_copy(cnt, cntv, ld_sem.at[6]),
    ]
    for load in loads:
        load.start()

    out_copies = []

    def remote(src, dst, sems, at, device):
        return pltpu.make_async_remote_copy(
            src_ref=src, dst_ref=dst, send_sem=sems[0].at[at[0]], recv_sem=sems[1].at[at[1]],
            device_id=device, device_id_type=MESH,
        )

    def send(copy):
        copy.start()

    def take(ref, sem):
        pltpu.make_async_copy(ref, ref, sem).wait()

    loads[1].wait()
    pl.semaphore_wait(barrier, len(partners))

    def origin(way, s):
        return (z - s + 8) % 8 if way == 0 else (z + s) % 8

    def w_copy(way, s, p, org):
        first, units, _ = W_GROUPS[p]
        rows = units * UNIT // 2
        rows_at = pl.ds(first * UNIT + way * rows, rows)
        ref = wg.at[org, rows_at]
        return remote(ref, ref, (ws, wr), ((way, p), (way, s, p)), (ahead, behind)[way])

    def h_copy(way, s, p, org):
        first, units, _ = H_GROUPS[p]
        ref = hg.at[org, pl.ds(first, units), pl.ds(way * 64, 64), :]
        return remote(ref, ref, (hs, hr), ((way, p), (way, s, p)), (ahead, behind)[way])

    def w_step(p, tick):
        s = tick - W_GROUPS[p][2]
        for way in range(2):
            if s >= 1:
                w_copy(way, s - 1, p, origin(way, s)).wait_recv()
                w_copy(way, s - 1, p, origin(way, s - 1)).wait_send()
            if s < STEPS:
                w_copy(way, s, p, origin(way, s)).start()

    def h_step(p, tick):
        s = tick - H_GROUPS[p][2]
        for way in range(2):
            if s >= 1:
                h_copy(way, s - 1, p, origin(way, s)).wait_recv()
                h_copy(way, s - 1, p, origin(way, s - 1)).wait_send()
            if s < STEPS:
                h_copy(way, s, p, origin(way, s)).start()

    for p in range(len(W_GROUPS)):
        w_step(p, 0)

    mine = 2 * c + xh
    my_rows = pl.ds(pl.multiple_of(g * 16, 16), 16)
    loads[0].wait()
    for xh_ in range(2):
        for z_ in range(NZ):
            for c_ in range(2):
                first = (xh_ * 16 + z_ * 2 + c_) * COL
                tp[2 * c_ + xh_, :, z_ * COL : (z_ + 1) * COL] = tv[:, first : first + COL]
    t1[mine] = tp[mine]
    my_cols = pl.ds(pl.multiple_of(z * COL, COL), COL)
    for s in range(4):
        t2[4 * z + s, my_rows, :] = tp[s, my_rows, my_cols]

    t1_to = ((core, 2 * (1 - c) + xh), (xnb[0], 2 * c + 1 - xh), (xnb[1], 2 * (1 - c) + 1 - xh))

    def t1_copy(j, slot):
        return remote(tp.at[t1_to[j][1]], t1.at[slot], (t1s, t1r), (0, 0), t1_to[j][0])

    def t2_across(k, at):
        cols = pl.ds(pl.multiple_of((z + k) % 8 * COL, COL), COL)
        return remote(
            tp.at[:, my_rows, cols], t2.at[pl.ds(4 * at, 4), my_rows, :],
            (t2as, t2ar), (0, 0), z_at(k),
        )

    def t2_among(k, owner):
        rows = pl.ds(pl.multiple_of(owner * 16, 16), 16)
        ref = t2.at[:, rows, :]
        return remote(ref, ref, (t2gs, t2gr), (0, 0), g_at(k))

    for j in range(3):
        send(t1_copy(j, mine))
    for k in range(1, 8):
        send(t2_across(k, z))

    ha_to = (xopp, core, core)

    def ha_copy(j, slot):
        ref = ha.at[slot]
        return remote(ref, ref, (has, har), (0, j), ha_to[j])

    loads[2].wait()
    loads[3].wait()
    for u in range(NU):
        cols = slice(u * UNIT, (u + 1) * UNIT)
        wide = gv[:, cols].astype(F32)
        hidden = (wide * jax.nn.sigmoid(wide) * uv[:, cols].astype(F32)).astype(BF16)
        hg[z, u] = hidden
        ha[mine, u] = hidden
    send(ha_copy(0, mine))
    send(ha_copy(1, mine))

    loads[4].wait()
    loads[5].wait()
    loads[6].wait()
    acc = jnp.zeros((TOK, 128), F32)
    for i in range(4):
        cols = pl.ds(pl.multiple_of(g * 512 + i * 128, 128), 128)
        acc += rv[:, i * 128 : (i + 1) * 128].astype(F32) * tv[:, cols].astype(F32)
    score_acc[...] = jnp.zeros_like(score_acc)
    score_acc[mine] = acc

    def hidden_pass_on():
        ha_copy(0, 2 * c + 1 - xh).wait_recv()
        send(ha_copy(2, 2 * c + 1 - xh))

    def hidden_here():
        ha_copy(1, 2 * (1 - c) + xh).wait_recv()
        ha_copy(2, 2 * (1 - c) + 1 - xh).wait_recv()

    def t2_pass_on():
        take(t2.at[pl.ds(0, 28), pl.ds(0, 16), :], t2ar.at[0])
        for k in range(1, 8):
            send(t2_among(k, g))

    def t2_turn():
        take(t2.at[:, pl.ds(0, 112), :], t2gr.at[0])

        def turn(i, carry):
            at = pl.ds(pl.multiple_of(i * TOK, TOK), TOK)
            for c_ in range(2):
                for xh_ in range(2):
                    block = t2[4 * i + 2 * c_ + xh_].astype(F32)
                    t2t[c_, xh_ * COL : (xh_ + 1) * COL, at] = block.T.astype(BF16)
            return carry

        lax.fori_loop(0, NZ, turn, 0)

    def t1_wait():
        take(t1.at[pl.ds(0, 3)], t1r.at[0])

    nt = (((1,), (1,)), ((), ()))

    def core_copy(u):
        return remote(cs.at[u], cr.at[u], (css, crs), (0, 0), core)

    def x_copy(u):
        return remote(xs.at[u], xr.at[u], (xss, xrs), (0, 0), xopp)

    def product(u):
        rows = pl.ds(u * UNIT, UNIT)
        block = jnp.concatenate([wg[i, rows, :] for i in range(NZ)], axis=1)
        for half, where in ((1 - c, None), (c, pm)):
            pair = pl.ds(2 * half, 2)
            lhs = t1[pair].reshape(2 * TOK, NZ * COL)
            out = lax.dot_general(lhs, block, nt, preferred_element_type=F32)
            out = out.reshape(2, TOK, UNIT)
            weighted = out * ha[pair, u].astype(F32)
            score_acc[pair] += weighted[:, :, :128] + weighted[:, :, 128:]
            if where is None:
                cs[u] = out.astype(BF16)
                send(core_copy(u))
            else:
                where[u] = out

    def across_x():
        take(cr, crs.at[0])
        for u in range(NU):
            xs[u] = (pm[u, 1 - xh] + cr[u, 1 - xh].astype(F32)).astype(BF16)
            send(x_copy(u))

    def back_of():
        take(xr, xrs.at[0])
        for u in range(NU):
            bk[u] = pm[u, xh] + cr[u, xh].astype(F32) + xr[u].astype(F32)

    lane = lax.broadcasted_iota(jnp.int32, (1, TOK), 1)

    def mask_row():
        return maskv[...].astype(F32)

    def sum_copy(k, owner):
        return remote(sb.at[owner], sb.at[owner], (sbs, sbr), (0, 0), g_at(k))

    def factor_copy(k, owner):
        return remote(fg.at[owner], fg.at[owner], (fgs, fgr), (0, 0), z_at(k))

    row_to = (
        (2 * (1 - c) + xh, core), (2 * c + 1 - xh, xopp), (2 * (1 - c) + 1 - xh, xopp2)
    )

    def row_copy(j):
        return remote(rb.at[j], rc.at[j], (rbs, rbr), (0, 0), row_to[j][1])

    def score_rows():
        for j in range(3):
            row = jnp.sum(score_acc[row_to[j][0]].T, axis=0, keepdims=True)
            rb[j] = jnp.broadcast_to(row, (8, TOK))
            send(row_copy(j))

    def sums():
        scores = jnp.sum(score_acc[mine].T, axis=0, keepdims=True)
        take(rc, rbr.at[0])
        scores = (scores + rc[0, 0:1, :] + rc[1, 0:1, :] + rc[2, 0:1, :]) * mask_row()
        first_sum = jnp.sum(jnp.where(lane < L, scores, 0.0), axis=1, keepdims=True)
        second_sum = jnp.sum(jnp.where(lane < L, 0.0, scores), axis=1, keepdims=True)
        row = lax.broadcasted_iota(jnp.int32, (8, 128), 0)
        sb[g] = jnp.where(row == 0, first_sum, second_sum)
        for k in range(1, 8):
            send(sum_copy(k, g))

    def factors():
        take(sb.at[pl.ds(0, 7)], sbr.at[0])
        total = sb[0]
        for i in range(1, 8):
            total = total + sb[i]
        count0 = cntv[0].astype(F32)
        count1 = cntv[1].astype(F32)
        reward0 = beta_coef * total[0:1, :] / count0
        reward1 = beta_coef * total[1:2, :] / count1
        margin = reward0 - reward1 - gamma_margin
        weight = jax.nn.sigmoid(-margin) * loss_scale * beta_coef
        factor = jnp.where(lane < L, -weight / count0, weight / count1) * mask_row()
        fg[z] = jnp.broadcast_to(factor, (8, 128))
        for k in range(1, 8):
            send(factor_copy(k, z))
        pair = jnp.maximum(-margin, 0.0) + jnp.log1p(jnp.exp(-jnp.abs(margin)))
        lossv[0] = pair[0, 0]
        out_copies.append(pltpu.make_async_copy(lossv, loss, out_sem.at[3]))
        out_copies[-1].start()

    def grads(first, units):
        by_row = jnp.broadcast_to(fg[z][0:1, :], (TOK, 128)).T
        by_row = jnp.concatenate([by_row, by_row], axis=1)
        for u in range(first, first + units):
            cols = slice(u * UNIT, (u + 1) * UNIT)
            wide = gv[:, cols].astype(F32)
            sig = jax.nn.sigmoid(wide)
            grad = by_row * bk[u]
            swish = wide * sig
            slope = sig + swish * (1.0 - sig)
            gg[:, cols] = (grad * uv[:, cols].astype(F32) * slope).astype(BF16)
            gu[:, cols] = (grad * swish).astype(BF16)

    def scaled():
        take(fg.at[pl.ds(0, 7)], fgr.at[0])

        def scale(i, carry):
            at = pl.ds(pl.multiple_of(i * TOK, TOK), TOK)
            by_lane = fg[i][0:1, :]
            for c_ in range(2):
                t2s[c_, :, at] = (t2t[c_, :, at].astype(F32) * by_lane).astype(BF16)
            return carry

        lax.fori_loop(0, NZ, scale, 0)

    nn = (((1,), (0,)), ((), ()))

    def core_copy2(u):
        return remote(cs2.at[u], cr2.at[u], (css2, crs2), (0, u), core)

    def x_copy2(u):
        return remote(xs2.at[u], xr2.at[u], (xss2, xrs2), (0, u), xopp)

    def product2(u):
        rhs = hg[:, u].reshape(NZ * TOK, UNIT)
        out = lax.dot_general(t2s[1 - c], rhs, nn, preferred_element_type=F32)
        cs2[u] = out.astype(BF16).reshape(2, COL, UNIT)
        send(core_copy2(u))
        out = lax.dot_general(t2s[c], rhs, nn, preferred_element_type=F32)
        dm[u] = out.reshape(2, COL, UNIT)

    def across_x2(u):
        core_copy2(u).wait_recv()
        xs2[u] = (dm[u, 1 - xh] + cr2[u, 1 - xh].astype(F32)).astype(BF16)
        send(x_copy2(u))

    def write(u):
        x_copy2(u).wait_recv()
        rows = pl.ds(u * UNIT, UNIT)
        gd[rows, :] = (dm[u, xh] + cr2[u, xh].astype(F32) + xr2[u].astype(F32)).T

    def flush():
        take(t1.at[pl.ds(0, 3)], t1s.at[0])
        take(t2.at[pl.ds(0, 28), pl.ds(0, 16), :], t2as.at[0])
        take(t2.at[:, pl.ds(0, 112), :], t2gs.at[0])
        take(ha.at[pl.ds(0, 3)], has.at[0])

    def flush_rest():
        take(rb, rbs.at[0])
        take(sb.at[pl.ds(0, 7)], sbs.at[0])
        take(fg.at[pl.ds(0, 7)], fgs.at[0])
        take(cs, css.at[0])
        take(xs, xss.at[0])

    tasks = {
        "W": w_step, "H": h_step, "pass": t2_pass_on, "turn": t2_turn, "t1": t1_wait,
        "P": product, "PX": across_x, "PB": back_of, "sum": sums, "factor": factors, "rows": score_rows, "hid": hidden_pass_on, "hids": hidden_here,
        "grad": grads, "scale": scaled, "D": product2, "DX": across_x2, "DO": write,
        "flush": flush, "rest": flush_rest,
    }
    for name, *given in SCHEDULE:
        tasks[name](*given)

    take(cs2, css2.at[0])
    take(xs2, xss2.at[0])
    for copy in out_copies:
        copy.wait()


def hand_over(*refs):
    sems = refs[-1]
    copies = [pltpu.make_async_copy(refs[i], refs[3 + i], sems.at[i]) for i in range(3)]
    for copy in copies:
        copy.start()
    for copy in copies:
        copy.wait()


def on_device(gate_pre, up_pre, down_weight, residual, target_rows, loss_mask, response_count):
    any_space = pl.BlockSpec(memory_space=pl.ANY)
    vmem = pl.BlockSpec(memory_space=pltpu.VMEM)
    sem = pltpu.SemaphoreType.DMA
    scratch = [
        pltpu.VMEM((TOK, HID), BF16),
        pltpu.VMEM((TOK, HID), BF16),
        pltpu.VMEM((TOK, 512), BF16),
        pltpu.VMEM((TOK, D), BF16),
        pltpu.VMEM((4, TOK, NZ * COL), BF16),
        pltpu.VMEM((4, TOK, NZ * COL), BF16),
        pltpu.VMEM((4 * NZ, TOK, COL), BF16),
        pltpu.VMEM((2, 2 * COL, NZ * TOK), BF16),
        pltpu.VMEM((2, 2 * COL, NZ * TOK), BF16),
        pltpu.VMEM((NZ, HID, COL), BF16),
        pltpu.VMEM((NZ, NU, TOK, UNIT), BF16),
        pltpu.VMEM((NU, 2, TOK, UNIT), F32),
        pltpu.VMEM((NU, 2, TOK, UNIT), BF16),
        pltpu.VMEM((NU, 2, TOK, UNIT), BF16),
        pltpu.VMEM((NU, TOK, UNIT), BF16),
        pltpu.VMEM((NU, TOK, UNIT), BF16),
        pltpu.VMEM((NU, TOK, UNIT), F32),
        pltpu.VMEM((NU, 2, COL, UNIT), F32),
        pltpu.VMEM((NU, 2, COL, UNIT), BF16),
        pltpu.VMEM((NU, 2, COL, UNIT), BF16),
        pltpu.VMEM((NU, COL, UNIT), BF16),
        pltpu.VMEM((NU, COL, UNIT), BF16),
        pltpu.VMEM((8, 8, 128), F32),
        pltpu.VMEM((8, 8, 128), F32),
        pltpu.VMEM((4, TOK, 128), F32),
        pltpu.VMEM((4, NU, TOK, UNIT), BF16),
        pltpu.VMEM((3, 8, TOK), F32),
        pltpu.VMEM((3, 8, TOK), F32),
        pltpu.VMEM((1, TOK), jnp.int32),
        pltpu.SMEM((2,), jnp.int32),
        pltpu.SMEM((1,), F32),
        sem((7,)),
        sem((4,)),
        sem((2, len(W_GROUPS))),
        sem((2, STEPS, len(W_GROUPS))),
        sem((2, len(H_GROUPS))),
        sem((2, STEPS, len(H_GROUPS))),
        *[sem((1,)) for _ in range(6)],
        *[sem((1,)) for _ in range(5)],
        sem((NU,)),
        sem((1,)),
        sem((NU,)),
        *[sem((1,)) for _ in range(4)],
        sem((1,)),
        sem((3,)),
        *[sem((1,)) for _ in range(2)],
    ]
    macs = 2 * 4 * TOK * NZ * COL * HID
    loss, grad_gate, grad_up, grad_down = pl.pallas_call(
        kernel,
        out_shape=(
            jax.ShapeDtypeStruct((1,), F32),
            pltpu.VMEM(gate_pre.shape, BF16),
            pltpu.VMEM(gate_pre.shape, BF16),
            pltpu.VMEM(down_weight.shape, F32),
        ),
        in_specs=[any_space] * 7,
        out_specs=(any_space, vmem, vmem, vmem),
        scratch_shapes=scratch,
        compiler_params=pltpu.CompilerParams(
            collective_id=0, has_side_effects=True, vmem_limit_bytes=56 << 20
        ),
        cost_estimate=pl.CostEstimate(flops=2 * macs, bytes_accessed=6 << 20, transcendentals=0),
    )(
        gate_pre, up_pre, down_weight, residual, target_rows,
        loss_mask.reshape(1, TOK), response_count,
    )
    grad_gate, grad_up, grad_down = pl.pallas_call(
        hand_over,
        out_shape=(
            jax.ShapeDtypeStruct(gate_pre.shape, BF16),
            jax.ShapeDtypeStruct(gate_pre.shape, BF16),
            jax.ShapeDtypeStruct(down_weight.shape, F32),
        ),
        in_specs=[vmem] * 3,
        out_specs=(any_space,) * 3,
        scratch_shapes=[sem((3,))],
    )(*[pltpu.with_memory_space_constraint(a, pltpu.VMEM) for a in (grad_gate, grad_up, grad_down)])
    return loss, grad_gate, grad_up, grad_down


def solution(mesh):
    placed = (
        P("fsdp", "tensor"),
        P("fsdp", "tensor"),
        P("tensor", "fsdp"),
        P("fsdp", None),
        P("fsdp", None),
        P("fsdp"),
        P("fsdp"),
    )
    return jax.shard_map(
        on_device,
        mesh=mesh,
        in_specs=placed,
        out_specs=(P("fsdp"), P("fsdp", "tensor"), P("fsdp", "tensor"), P("tensor", "fsdp")),
        check_vma=False,
    )
```

```python
import functools

import jax
import jax.numpy as jnp
from jax import lax
from jax.experimental import pallas as pl
from jax.experimental.pallas import tpu as pltpu
from jax.sharding import PartitionSpec as P

MESH = pl.DeviceIdType.MESH
F32 = jnp.float32
BF16 = jnp.bfloat16

beta_coef = 2.0
gamma_margin = 1.0
loss_scale = 1024.0

L = 64
NZ = 8
TOK = 128
COL = 128
UNIT = 256
NU = 7
HID = UNIT * NU
D = 4096

W_GROUPS = ((0, 4, 0), (4, 3, 0))
H_GROUPS = ((0, 2, 2), (2, 2, 3), (4, 2, 4), (6, 1, 4))
STEPS = NZ // 2


EARLY = {
    (1, "W", 1): [("pass",), ("hid",)],
    (2, "W", 1): [("turn",)],
    (3, "W", 1): [("t1",), ("hids",)],
    (4, "W", 0): [("P", 0), ("P", 1), ("P", 2), ("P", 3)],
    (4, "W", 1): [("P", 4), ("P", 5), ("P", 6), ("rows",)],
}


def make_schedule():
    after = dict(EARLY)
    last = len(H_GROUPS) - 1
    ends = [begin + STEPS for _, _, begin in H_GROUPS]
    after[4, "H", last] = [("sum",), ("flush",)]
    after[5, "H", 0] = [("factor",)]
    after[5, "H", 1] = [("PX",)]
    after[5, "H", last] = [("scale",)]
    for tick in sorted(set(ends)):
        units = [u for p, e in enumerate(ends) if e == tick for u in range(H_GROUPS[p][0], H_GROUPS[p][0] + H_GROUPS[p][1])]
        todo = after.setdefault((tick, "H", last), [])
        todo += [("D", u) for u in units]
        todo += [("PB",), ("grad", 0, 7)] if tick == 6 else []
        todo += [("rest",)] if tick == ends[-1] else []
        todo += [("DX", u) for u in units]
    todo += [("DO", u) for u in range(NU)]
    order = []
    for tick in range(ends[-1] + 1):
        for kind, groups in (("W", W_GROUPS), ("H", H_GROUPS)):
            for p, (_, _, begin) in enumerate(groups):
                if begin <= tick <= begin + STEPS and (tick > 0 or kind != "W"):
                    order.append((kind, p, tick))
                order += after.get((tick, kind, p), [])
    return order


SCHEDULE = make_schedule()


def kernel(
    gate, up, w, resid, tgt, mask, cnt, loss, gg, gu, gd,
    gv, uv, rv, tv, tp, t1, t2, t2t, t2s, wg, hg, pm, cs, cr, xs, xr, bk,
    dm, cs2, cr2, xs2, xr2, sb, fg, score_acc, ha, rb, rc, maskv, cntv, lossv,
    ld_sem, out_sem, ws, wr, hs, hr, t1s, t1r, t2as, t2ar, t2gs, t2gr,
    css, crs, xss, xrs, css2, crs2, xss2, xrs2, sbs, sbr, fgs, fgr, has, har, rbs, rbr,
):
    f = lax.axis_index("fsdp")
    g = lax.axis_index("tensor")
    xh, z, c = f // 16, (f // 2) % 8, f % 2
    xl, y = g // 4, g % 4

    def place(xh_, z_, c_, xl_=xl, y_=y):
        return (xh_ * 16 + z_ * 2 + c_, xl_ * 4 + y_)

    def z_at(k):
        return (f // 16 * 16 + (z + k) % 8 * 2 + c, g)

    def g_at(k):
        return (f, (g + k) % 8)

    core = place(xh, z, 1 - c)
    xopp = place(1 - xh, z, c)
    xopp2 = place(1 - xh, z, 1 - c)
    xnb = (place(1 - xh, z, c, 1 - xl), place(1 - xh, z, 1 - c, 1 - xl))
    ahead, behind = z_at(1), z_at(7)

    barrier = pltpu.get_barrier_semaphore()
    partners = [z_at(k) for k in range(1, 8)] + [g_at(k) for k in range(1, 8)]
    partners += [core, xopp, xopp2, *xnb]
    for partner in partners:
        pl.semaphore_signal(barrier, inc=1, device_id=partner, device_id_type=MESH)

    loads = [
        pltpu.make_async_copy(tgt, tv, ld_sem.at[0]),
        pltpu.make_async_copy(w, wg.at[z], ld_sem.at[1]),
        pltpu.make_async_copy(gate, gv, ld_sem.at[2]),
        pltpu.make_async_copy(up, uv, ld_sem.at[3]),
        pltpu.make_async_copy(
            resid.at[:, pl.ds(pl.multiple_of(g * 512, 512), 512)], rv, ld_sem.at[4]
        ),
        pltpu.make_async_copy(mask, maskv, ld_sem.at[5]),
        pltpu.make_async_copy(cnt, cntv, ld_sem.at[6]),
    ]
    for load in loads:
        load.start()

    out_copies = []

    def remote(src, dst, sems, at, device):
        return pltpu.make_async_remote_copy(
            src_ref=src, dst_ref=dst, send_sem=sems[0].at[at[0]], recv_sem=sems[1].at[at[1]],
            device_id=device, device_id_type=MESH,
        )

    def send(copy):
        copy.start()

    def take(ref, sem):
        pltpu.make_async_copy(ref, ref, sem).wait()

    loads[1].wait()
    pl.semaphore_wait(barrier, len(partners))

    def origin(way, s):
        return (z - s + 8) % 8 if way == 0 else (z + s) % 8

    def w_copy(way, s, p, org):
        first, units, _ = W_GROUPS[p]
        rows, start = units * UNIT, first * UNIT
        if s == STEPS - 1:
            rows, start = rows // 2, start + way * rows // 2
        rows_at = pl.ds(start, rows)
        ref = wg.at[org, rows_at]
        return remote(ref, ref, (ws, wr), ((way, p), (way, s, p)), (ahead, behind)[way])

    def h_copy(way, s, p, org):
        first, units, _ = H_GROUPS[p]
        rows = pl.ds(way * 64, 64) if s == STEPS - 1 else pl.ds(0, TOK)
        ref = hg.at[org, pl.ds(first, units), rows, :]
        return remote(ref, ref, (hs, hr), ((way, p), (way, s, p)), (ahead, behind)[way])

    def w_step(p, tick):
        s = tick - W_GROUPS[p][2]
        for way in range(2):
            if s >= 1:
                w_copy(way, s - 1, p, origin(way, s)).wait_recv()
                w_copy(way, s - 1, p, origin(way, s - 1)).wait_send()
            if s < STEPS:
                w_copy(way, s, p, origin(way, s)).start()

    def h_step(p, tick):
        s = tick - H_GROUPS[p][2]
        for way in range(2):
            if s >= 1:
                h_copy(way, s - 1, p, origin(way, s)).wait_recv()
                h_copy(way, s - 1, p, origin(way, s - 1)).wait_send()
            if s < STEPS:
                h_copy(way, s, p, origin(way, s)).start()

    for p in range(len(W_GROUPS)):
        w_step(p, 0)

    mine = 2 * c + xh
    my_rows = pl.ds(pl.multiple_of(g * 16, 16), 16)
    loads[0].wait()
    for xh_ in range(2):
        for z_ in range(NZ):
            for c_ in range(2):
                first = (xh_ * 16 + z_ * 2 + c_) * COL
                tp[2 * c_ + xh_, :, z_ * COL : (z_ + 1) * COL] = tv[:, first : first + COL]
    t1[mine] = tp[mine]
    my_cols = pl.ds(pl.multiple_of(z * COL, COL), COL)
    for s in range(4):
        t2[4 * z + s, my_rows, :] = tp[s, my_rows, my_cols]

    t1_to = ((core, 2 * (1 - c) + xh), (xnb[0], 2 * c + 1 - xh), (xnb[1], 2 * (1 - c) + 1 - xh))

    def t1_copy(j, slot):
        return remote(tp.at[t1_to[j][1]], t1.at[slot], (t1s, t1r), (0, 0), t1_to[j][0])

    def t2_across(k, at):
        cols = pl.ds(pl.multiple_of((z + k) % 8 * COL, COL), COL)
        return remote(
            tp.at[:, my_rows, cols], t2.at[pl.ds(4 * at, 4), my_rows, :],
            (t2as, t2ar), (0, 0), z_at(k),
        )

    def t2_among(k, owner):
        rows = pl.ds(pl.multiple_of(owner * 16, 16), 16)
        ref = t2.at[:, rows, :]
        return remote(ref, ref, (t2gs, t2gr), (0, 0), g_at(k))

    for j in range(3):
        send(t1_copy(j, mine))
    for k in range(1, 8):
        send(t2_across(k, z))

    ha_to = (xopp, core, core)

    def ha_copy(j, slot):
        ref = ha.at[slot]
        return remote(ref, ref, (has, har), (0, j), ha_to[j])

    loads[2].wait()
    loads[3].wait()
    for u in range(NU):
        cols = slice(u * UNIT, (u + 1) * UNIT)
        wide = gv[:, cols].astype(F32)
        hidden = (wide * jax.nn.sigmoid(wide) * uv[:, cols].astype(F32)).astype(BF16)
        hg[z, u] = hidden
        ha[mine, u] = hidden
    send(ha_copy(0, mine))
    send(ha_copy(1, mine))

    loads[4].wait()
    loads[5].wait()
    loads[6].wait()
    acc = jnp.zeros((TOK, 128), F32)
    for i in range(4):
        cols = pl.ds(pl.multiple_of(g * 512 + i * 128, 128), 128)
        acc += rv[:, i * 128 : (i + 1) * 128].astype(F32) * tv[:, cols].astype(F32)
    score_acc[...] = jnp.zeros_like(score_acc)
    score_acc[mine] = acc

    def hidden_pass_on():
        ha_copy(0, 2 * c + 1 - xh).wait_recv()
        send(ha_copy(2, 2 * c + 1 - xh))

    def hidden_here():
        ha_copy(1, 2 * (1 - c) + xh).wait_recv()
        ha_copy(2, 2 * (1 - c) + 1 - xh).wait_recv()

    def t2_pass_on():
        take(t2.at[pl.ds(0, 28), pl.ds(0, 16), :], t2ar.at[0])
        for k in range(1, 8):
            send(t2_among(k, g))

    def t2_turn():
        take(t2.at[:, pl.ds(0, 112), :], t2gr.at[0])

        def turn(i, carry):
            at = pl.ds(pl.multiple_of(i * TOK, TOK), TOK)
            for c_ in range(2):
                for xh_ in range(2):
                    block = t2[4 * i + 2 * c_ + xh_].astype(F32)
                    t2t[c_, xh_ * COL : (xh_ + 1) * COL, at] = block.T.astype(BF16)
            return carry

        lax.fori_loop(0, NZ, turn, 0)

    def t1_wait():
        take(t1.at[pl.ds(0, 3)], t1r.at[0])

    nt = (((1,), (1,)), ((), ()))

    def core_copy(u):
        return remote(cs.at[u], cr.at[u], (css, crs), (0, 0), core)

    def x_copy(u):
        return remote(xs.at[u], xr.at[u], (xss, xrs), (0, 0), xopp)

    def product(u):
        rows = pl.ds(u * UNIT, UNIT)
        block = jnp.concatenate([wg[i, rows, :] for i in range(NZ)], axis=1)
        for half, where in ((1 - c, None), (c, pm)):
            pair = pl.ds(2 * half, 2)
            lhs = t1[pair].reshape(2 * TOK, NZ * COL)
            out = lax.dot_general(lhs, block, nt, preferred_element_type=F32)
            out = out.reshape(2, TOK, UNIT)
            weighted = out * ha[pair, u].astype(F32)
            score_acc[pair] += weighted[:, :, :128] + weighted[:, :, 128:]
            if where is None:
                cs[u] = out.astype(BF16)
                send(core_copy(u))
            else:
                where[u] = out

    def across_x():
        take(cr, crs.at[0])
        for u in range(NU):
            xs[u] = (pm[u, 1 - xh] + cr[u, 1 - xh].astype(F32)).astype(BF16)
            send(x_copy(u))

    def back_of():
        take(xr, xrs.at[0])
        for u in range(NU):
            bk[u] = pm[u, xh] + cr[u, xh].astype(F32) + xr[u].astype(F32)

    lane = lax.broadcasted_iota(jnp.int32, (1, TOK), 1)

    def mask_row():
        return maskv[...].astype(F32)

    def sum_copy(k, owner):
        return remote(sb.at[owner], sb.at[owner], (sbs, sbr), (0, 0), g_at(k))

    def factor_copy(k, owner):
        return remote(fg.at[owner], fg.at[owner], (fgs, fgr), (0, 0), z_at(k))

    row_to = (
        (2 * (1 - c) + xh, core), (2 * c + 1 - xh, xopp), (2 * (1 - c) + 1 - xh, xopp2)
    )

    def row_copy(j):
        return remote(rb.at[j], rc.at[j], (rbs, rbr), (0, 0), row_to[j][1])

    def score_rows():
        for j in range(3):
            row = jnp.sum(score_acc[row_to[j][0]].T, axis=0, keepdims=True)
            rb[j] = jnp.broadcast_to(row, (8, TOK))
            send(row_copy(j))

    def sums():
        scores = jnp.sum(score_acc[mine].T, axis=0, keepdims=True)
        take(rc, rbr.at[0])
        scores = (scores + rc[0, 0:1, :] + rc[1, 0:1, :] + rc[2, 0:1, :]) * mask_row()
        first_sum = jnp.sum(jnp.where(lane < L, scores, 0.0), axis=1, keepdims=True)
        second_sum = jnp.sum(jnp.where(lane < L, 0.0, scores), axis=1, keepdims=True)
        row = lax.broadcasted_iota(jnp.int32, (8, 128), 0)
        sb[g] = jnp.where(row == 0, first_sum, second_sum)
        for k in range(1, 8):
            send(sum_copy(k, g))

    def factors():
        take(sb.at[pl.ds(0, 7)], sbr.at[0])
        total = sb[0]
        for i in range(1, 8):
            total = total + sb[i]
        count0 = cntv[0].astype(F32)
        count1 = cntv[1].astype(F32)
        reward0 = beta_coef * total[0:1, :] / count0
        reward1 = beta_coef * total[1:2, :] / count1
        margin = reward0 - reward1 - gamma_margin
        weight = jax.nn.sigmoid(-margin) * loss_scale * beta_coef
        factor = jnp.where(lane < L, -weight / count0, weight / count1) * mask_row()
        fg[z] = jnp.broadcast_to(factor, (8, 128))
        for k in range(1, 8):
            send(factor_copy(k, z))
        pair = jnp.maximum(-margin, 0.0) + jnp.log1p(jnp.exp(-jnp.abs(margin)))
        lossv[0] = pair[0, 0]
        out_copies.append(pltpu.make_async_copy(lossv, loss, out_sem.at[3]))
        out_copies[-1].start()

    def grads(first, units):
        by_row = jnp.broadcast_to(fg[z][0:1, :], (TOK, 128)).T
        by_row = jnp.concatenate([by_row, by_row], axis=1)
        for u in range(first, first + units):
            cols = slice(u * UNIT, (u + 1) * UNIT)
            wide = gv[:, cols].astype(F32)
            sig = jax.nn.sigmoid(wide)
            grad = by_row * bk[u]
            swish = wide * sig
            slope = sig + swish * (1.0 - sig)
            gg[:, cols] = (grad * uv[:, cols].astype(F32) * slope).astype(BF16)
            gu[:, cols] = (grad * swish).astype(BF16)

    def scaled():
        take(fg.at[pl.ds(0, 7)], fgr.at[0])

        def scale(i, carry):
            at = pl.ds(pl.multiple_of(i * TOK, TOK), TOK)
            by_lane = fg[i][0:1, :]
            for c_ in range(2):
                t2s[c_, :, at] = (t2t[c_, :, at].astype(F32) * by_lane).astype(BF16)
            return carry

        lax.fori_loop(0, NZ, scale, 0)

    nn = (((1,), (0,)), ((), ()))

    def core_copy2(u):
        return remote(cs2.at[u], cr2.at[u], (css2, crs2), (0, u), core)

    def x_copy2(u):
        return remote(xs2.at[u], xr2.at[u], (xss2, xrs2), (0, u), xopp)

    def product2(u):
        rhs = hg[:, u].reshape(NZ * TOK, UNIT)
        out = lax.dot_general(t2s[1 - c], rhs, nn, preferred_element_type=F32)
        cs2[u] = out.astype(BF16).reshape(2, COL, UNIT)
        send(core_copy2(u))
        out = lax.dot_general(t2s[c], rhs, nn, preferred_element_type=F32)
        dm[u] = out.reshape(2, COL, UNIT)

    def across_x2(u):
        core_copy2(u).wait_recv()
        xs2[u] = (dm[u, 1 - xh] + cr2[u, 1 - xh].astype(F32)).astype(BF16)
        send(x_copy2(u))

    def write(u):
        x_copy2(u).wait_recv()
        rows = pl.ds(u * UNIT, UNIT)
        gd[rows, :] = (dm[u, xh] + cr2[u, xh].astype(F32) + xr2[u].astype(F32)).T

    def flush():
        take(t1.at[pl.ds(0, 3)], t1s.at[0])
        take(t2.at[pl.ds(0, 28), pl.ds(0, 16), :], t2as.at[0])
        take(t2.at[:, pl.ds(0, 112), :], t2gs.at[0])
        take(ha.at[pl.ds(0, 3)], has.at[0])

    def flush_rest():
        take(rb, rbs.at[0])
        take(sb.at[pl.ds(0, 7)], sbs.at[0])
        take(fg.at[pl.ds(0, 7)], fgs.at[0])
        take(cs, css.at[0])
        take(xs, xss.at[0])

    tasks = {
        "W": w_step, "H": h_step, "pass": t2_pass_on, "turn": t2_turn, "t1": t1_wait,
        "P": product, "PX": across_x, "PB": back_of, "sum": sums, "factor": factors, "rows": score_rows, "hid": hidden_pass_on, "hids": hidden_here,
        "grad": grads, "scale": scaled, "D": product2, "DX": across_x2, "DO": write,
        "flush": flush, "rest": flush_rest,
    }
    for name, *given in SCHEDULE:
        tasks[name](*given)

    take(cs2, css2.at[0])
    take(xs2, xss2.at[0])
    for copy in out_copies:
        copy.wait()


def hand_over(*refs):
    sems = refs[-1]
    copies = [pltpu.make_async_copy(refs[i], refs[3 + i], sems.at[i]) for i in range(3)]
    for copy in copies:
        copy.start()
    for copy in copies:
        copy.wait()


def on_device(gate_pre, up_pre, down_weight, residual, target_rows, loss_mask, response_count):
    any_space = pl.BlockSpec(memory_space=pl.ANY)
    vmem = pl.BlockSpec(memory_space=pltpu.VMEM)
    sem = pltpu.SemaphoreType.DMA
    scratch = [
        pltpu.VMEM((TOK, HID), BF16),
        pltpu.VMEM((TOK, HID), BF16),
        pltpu.VMEM((TOK, 512), BF16),
        pltpu.VMEM((TOK, D), BF16),
        pltpu.VMEM((4, TOK, NZ * COL), BF16),
        pltpu.VMEM((4, TOK, NZ * COL), BF16),
        pltpu.VMEM((4 * NZ, TOK, COL), BF16),
        pltpu.VMEM((2, 2 * COL, NZ * TOK), BF16),
        pltpu.VMEM((2, 2 * COL, NZ * TOK), BF16),
        pltpu.VMEM((NZ, HID, COL), BF16),
        pltpu.VMEM((NZ, NU, TOK, UNIT), BF16),
        pltpu.VMEM((NU, 2, TOK, UNIT), F32),
        pltpu.VMEM((NU, 2, TOK, UNIT), BF16),
        pltpu.VMEM((NU, 2, TOK, UNIT), BF16),
        pltpu.VMEM((NU, TOK, UNIT), BF16),
        pltpu.VMEM((NU, TOK, UNIT), BF16),
        pltpu.VMEM((NU, TOK, UNIT), F32),
        pltpu.VMEM((NU, 2, COL, UNIT), F32),
        pltpu.VMEM((NU, 2, COL, UNIT), BF16),
        pltpu.VMEM((NU, 2, COL, UNIT), BF16),
        pltpu.VMEM((NU, COL, UNIT), BF16),
        pltpu.VMEM((NU, COL, UNIT), BF16),
        pltpu.VMEM((8, 8, 128), F32),
        pltpu.VMEM((8, 8, 128), F32),
        pltpu.VMEM((4, TOK, 128), F32),
        pltpu.VMEM((4, NU, TOK, UNIT), BF16),
        pltpu.VMEM((3, 8, TOK), F32),
        pltpu.VMEM((3, 8, TOK), F32),
        pltpu.VMEM((1, TOK), jnp.int32),
        pltpu.SMEM((2,), jnp.int32),
        pltpu.SMEM((1,), F32),
        sem((7,)),
        sem((4,)),
        sem((2, len(W_GROUPS))),
        sem((2, STEPS, len(W_GROUPS))),
        sem((2, len(H_GROUPS))),
        sem((2, STEPS, len(H_GROUPS))),
        *[sem((1,)) for _ in range(6)],
        *[sem((1,)) for _ in range(5)],
        sem((NU,)),
        sem((1,)),
        sem((NU,)),
        *[sem((1,)) for _ in range(4)],
        sem((1,)),
        sem((3,)),
        *[sem((1,)) for _ in range(2)],
    ]
    macs = 2 * 4 * TOK * NZ * COL * HID
    loss, grad_gate, grad_up, grad_down = pl.pallas_call(
        kernel,
        out_shape=(
            jax.ShapeDtypeStruct((1,), F32),
            pltpu.VMEM(gate_pre.shape, BF16),
            pltpu.VMEM(gate_pre.shape, BF16),
            pltpu.VMEM(down_weight.shape, F32),
        ),
        in_specs=[any_space] * 7,
        out_specs=(any_space, vmem, vmem, vmem),
        scratch_shapes=scratch,
        compiler_params=pltpu.CompilerParams(
            collective_id=0, has_side_effects=True, vmem_limit_bytes=56 << 20
        ),
        cost_estimate=pl.CostEstimate(flops=2 * macs, bytes_accessed=6 << 20, transcendentals=0),
    )(
        gate_pre, up_pre, down_weight, residual, target_rows,
        loss_mask.reshape(1, TOK), response_count,
    )
    grad_gate, grad_up, grad_down = pl.pallas_call(
        hand_over,
        out_shape=(
            jax.ShapeDtypeStruct(gate_pre.shape, BF16),
            jax.ShapeDtypeStruct(gate_pre.shape, BF16),
            jax.ShapeDtypeStruct(down_weight.shape, F32),
        ),
        in_specs=[vmem] * 3,
        out_specs=(any_space,) * 3,
        scratch_shapes=[sem((3,))],
    )(*[pltpu.with_memory_space_constraint(a, pltpu.VMEM) for a in (grad_gate, grad_up, grad_down)])
    return loss, grad_gate, grad_up, grad_down


def solution(mesh):
    placed = (
        P("fsdp", "tensor"),
        P("fsdp", "tensor"),
        P("tensor", "fsdp"),
        P("fsdp", None),
        P("fsdp", None),
        P("fsdp"),
        P("fsdp"),
    )
    return jax.shard_map(
        on_device,
        mesh=mesh,
        in_specs=placed,
        out_specs=(P("fsdp"), P("fsdp", "tensor"), P("fsdp", "tensor"), P("tensor", "fsdp")),
        check_vma=False,
    )
```

```python
import functools

import jax
import jax.numpy as jnp
from jax import lax
from jax.experimental import pallas as pl
from jax.experimental.pallas import tpu as pltpu
from jax.sharding import PartitionSpec as P

MESH = pl.DeviceIdType.MESH
F32 = jnp.float32
BF16 = jnp.bfloat16

beta_coef = 2.0
gamma_margin = 1.0
loss_scale = 1024.0

L = 64
NZ = 8
TOK = 128
COL = 128
UNIT = 256
NU = 7
HID = UNIT * NU
D = 4096

W_GROUPS = ((0, 4, 0), (4, 3, 0))
H_GROUPS = ((0, 2, 2), (2, 2, 3), (4, 2, 4), (6, 1, 4))
STEPS = NZ // 2


EARLY = {
    (1, "W", 1): [("pass",), ("hid",)],
    (2, "W", 1): [("turn",)],
    (3, "W", 1): [("t1",), ("hids",)],
    (4, "W", 0): [("P", 0), ("P", 1), ("P", 2), ("P", 3)],
    (4, "W", 1): [("P", 4), ("P", 5), ("P", 6), ("rows",)],
}


def make_schedule():
    after = dict(EARLY)
    last = len(H_GROUPS) - 1
    ends = [begin + STEPS for _, _, begin in H_GROUPS]
    after[4, "H", last] = [("sum",), ("flush",)]
    after[5, "H", 0] = [("factor",)]
    after[5, "H", 1] = [("PX",)]
    after[5, "H", last] = [("scale",)]
    for tick in sorted(set(ends)):
        units = [u for p, e in enumerate(ends) if e == tick for u in range(H_GROUPS[p][0], H_GROUPS[p][0] + H_GROUPS[p][1])]
        todo = after.setdefault((tick, "H", last), [])
        if tick == ends[-1]:
            after[tick, "H", last - 1] = [("D", u) for u in units[:-1]]
            units = units[-1:]
        todo += [("D", u) for u in units]
        todo += [("PB",), ("grad", 0, 7)] if tick == 6 else []
        todo += [("rest",)] if tick == ends[-1] else []
        todo += [("DX", u) for u in (units if tick < ends[-1] else (4, 5, 6))]
    todo += [("DO", u) for u in range(NU)]
    order = []
    for tick in range(ends[-1] + 1):
        for kind, groups in (("W", W_GROUPS), ("H", H_GROUPS)):
            for p, (_, _, begin) in enumerate(groups):
                if begin <= tick <= begin + STEPS and (tick > 0 or kind != "W"):
                    order.append((kind, p, tick))
                order += after.get((tick, kind, p), [])
    return order


SCHEDULE = make_schedule()


def kernel(
    gate, up, w, resid, tgt, mask, cnt, loss, gg, gu, gd,
    gv, uv, rv, tv, tp, t1, t2, t2t, t2s, wg, hg, pm, cs, cr, xs, xr, bk,
    dm, cs2, cr2, xs2, xr2, sb, fg, score_acc, ha, rb, rc, maskv, cntv, lossv,
    ld_sem, out_sem, ws, wr, hs, hr, t1s, t1r, t2as, t2ar, t2gs, t2gr,
    css, crs, xss, xrs, css2, crs2, xss2, xrs2, sbs, sbr, fgs, fgr, has, har, rbs, rbr,
):
    f = lax.axis_index("fsdp")
    g = lax.axis_index("tensor")
    xh, z, c = f // 16, (f // 2) % 8, f % 2
    xl, y = g // 4, g % 4

    def place(xh_, z_, c_, xl_=xl, y_=y):
        return (xh_ * 16 + z_ * 2 + c_, xl_ * 4 + y_)

    def z_at(k):
        return (f // 16 * 16 + (z + k) % 8 * 2 + c, g)

    def g_at(k):
        return (f, (g + k) % 8)

    core = place(xh, z, 1 - c)
    xopp = place(1 - xh, z, c)
    xopp2 = place(1 - xh, z, 1 - c)
    xnb = (place(1 - xh, z, c, 1 - xl), place(1 - xh, z, 1 - c, 1 - xl))
    ahead, behind = z_at(1), z_at(7)

    barrier = pltpu.get_barrier_semaphore()
    partners = [z_at(k) for k in range(1, 8)] + [g_at(k) for k in range(1, 8)]
    partners += [core, xopp, xopp2, *xnb]
    for partner in partners:
        pl.semaphore_signal(barrier, inc=1, device_id=partner, device_id_type=MESH)

    loads = [
        pltpu.make_async_copy(tgt, tv, ld_sem.at[0]),
        pltpu.make_async_copy(w, wg.at[z], ld_sem.at[1]),
        pltpu.make_async_copy(gate, gv, ld_sem.at[2]),
        pltpu.make_async_copy(up, uv, ld_sem.at[3]),
        pltpu.make_async_copy(
            resid.at[:, pl.ds(pl.multiple_of(g * 512, 512), 512)], rv, ld_sem.at[4]
        ),
        pltpu.make_async_copy(mask, maskv, ld_sem.at[5]),
        pltpu.make_async_copy(cnt, cntv, ld_sem.at[6]),
    ]
    for load in loads:
        load.start()

    out_copies = []

    def remote(src, dst, sems, at, device):
        return pltpu.make_async_remote_copy(
            src_ref=src, dst_ref=dst, send_sem=sems[0].at[at[0]], recv_sem=sems[1].at[at[1]],
            device_id=device, device_id_type=MESH,
        )

    def send(copy):
        copy.start()

    def take(ref, sem):
        pltpu.make_async_copy(ref, ref, sem).wait()

    loads[1].wait()
    pl.semaphore_wait(barrier, len(partners))

    def origin(way, s):
        return (z - s + 8) % 8 if way == 0 else (z + s) % 8

    def w_copy(way, s, p, org):
        first, units, _ = W_GROUPS[p]
        rows, start = units * UNIT, first * UNIT
        if s == STEPS - 1:
            rows, start = rows // 2, start + way * rows // 2
        rows_at = pl.ds(start, rows)
        ref = wg.at[org, rows_at]
        return remote(ref, ref, (ws, wr), ((way, p), (way, s, p)), (ahead, behind)[way])

    def h_copy(way, s, p, org):
        first, units, _ = H_GROUPS[p]
        rows = pl.ds(way * 64, 64) if s == STEPS - 1 else pl.ds(0, TOK)
        ref = hg.at[org, pl.ds(first, units), rows, :]
        return remote(ref, ref, (hs, hr), ((way, p), (way, s, p)), (ahead, behind)[way])

    def w_step(p, tick):
        s = tick - W_GROUPS[p][2]
        for way in range(2):
            if s >= 1:
                w_copy(way, s - 1, p, origin(way, s)).wait_recv()
                w_copy(way, s - 1, p, origin(way, s - 1)).wait_send()
            if s < STEPS:
                w_copy(way, s, p, origin(way, s)).start()

    def h_step(p, tick):
        s = tick - H_GROUPS[p][2]
        for way in range(2):
            if s >= 1:
                h_copy(way, s - 1, p, origin(way, s)).wait_recv()
                h_copy(way, s - 1, p, origin(way, s - 1)).wait_send()
            if s < STEPS:
                h_copy(way, s, p, origin(way, s)).start()

    for p in range(len(W_GROUPS)):
        w_step(p, 0)

    mine = 2 * c + xh
    my_rows = pl.ds(pl.multiple_of(g * 16, 16), 16)
    loads[0].wait()
    for xh_ in range(2):
        for z_ in range(NZ):
            for c_ in range(2):
                first = (xh_ * 16 + z_ * 2 + c_) * COL
                tp[2 * c_ + xh_, :, z_ * COL : (z_ + 1) * COL] = tv[:, first : first + COL]
    t1[mine] = tp[mine]
    my_cols = pl.ds(pl.multiple_of(z * COL, COL), COL)
    for s in range(4):
        t2[4 * z + s, my_rows, :] = tp[s, my_rows, my_cols]

    t1_to = ((core, 2 * (1 - c) + xh), (xnb[0], 2 * c + 1 - xh), (xnb[1], 2 * (1 - c) + 1 - xh))

    def t1_copy(j, slot):
        return remote(tp.at[t1_to[j][1]], t1.at[slot], (t1s, t1r), (0, 0), t1_to[j][0])

    def t2_across(k, at):
        cols = pl.ds(pl.multiple_of((z + k) % 8 * COL, COL), COL)
        return remote(
            tp.at[:, my_rows, cols], t2.at[pl.ds(4 * at, 4), my_rows, :],
            (t2as, t2ar), (0, 0), z_at(k),
        )

    def t2_among(k, owner):
        rows = pl.ds(pl.multiple_of(owner * 16, 16), 16)
        ref = t2.at[:, rows, :]
        return remote(ref, ref, (t2gs, t2gr), (0, 0), g_at(k))

    for j in range(3):
        send(t1_copy(j, mine))
    for k in range(1, 8):
        send(t2_across(k, z))

    ha_to = (xopp, core, core)

    def ha_copy(j, slot):
        ref = ha.at[slot]
        return remote(ref, ref, (has, har), (0, j), ha_to[j])

    loads[2].wait()
    loads[3].wait()
    for u in range(NU):
        cols = slice(u * UNIT, (u + 1) * UNIT)
        wide = gv[:, cols].astype(F32)
        hidden = (wide * jax.nn.sigmoid(wide) * uv[:, cols].astype(F32)).astype(BF16)
        hg[z, u] = hidden
        ha[mine, u] = hidden
    send(ha_copy(0, mine))
    send(ha_copy(1, mine))

    loads[4].wait()
    loads[5].wait()
    loads[6].wait()
    acc = jnp.zeros((TOK, 128), F32)
    for i in range(4):
        cols = pl.ds(pl.multiple_of(g * 512 + i * 128, 128), 128)
        acc += rv[:, i * 128 : (i + 1) * 128].astype(F32) * tv[:, cols].astype(F32)
    score_acc[...] = jnp.zeros_like(score_acc)
    score_acc[mine] = acc

    def hidden_pass_on():
        ha_copy(0, 2 * c + 1 - xh).wait_recv()
        send(ha_copy(2, 2 * c + 1 - xh))

    def hidden_here():
        ha_copy(1, 2 * (1 - c) + xh).wait_recv()
        ha_copy(2, 2 * (1 - c) + 1 - xh).wait_recv()

    def t2_pass_on():
        take(t2.at[pl.ds(0, 28), pl.ds(0, 16), :], t2ar.at[0])
        for k in range(1, 8):
            send(t2_among(k, g))

    def t2_turn():
        take(t2.at[:, pl.ds(0, 112), :], t2gr.at[0])

        def turn(i, carry):
            at = pl.ds(pl.multiple_of(i * TOK, TOK), TOK)
            for c_ in range(2):
                for xh_ in range(2):
                    block = t2[4 * i + 2 * c_ + xh_].astype(F32)
                    t2t[c_, xh_ * COL : (xh_ + 1) * COL, at] = block.T.astype(BF16)
            return carry

        lax.fori_loop(0, NZ, turn, 0)

    def t1_wait():
        take(t1.at[pl.ds(0, 3)], t1r.at[0])

    nt = (((1,), (1,)), ((), ()))

    def core_copy(u):
        return remote(cs.at[u], cr.at[u], (css, crs), (0, 0), core)

    def x_copy(u):
        return remote(xs.at[u], xr.at[u], (xss, xrs), (0, 0), xopp)

    def product(u):
        rows = pl.ds(u * UNIT, UNIT)
        block = jnp.concatenate([wg[i, rows, :] for i in range(NZ)], axis=1)
        for half, where in ((1 - c, None), (c, pm)):
            pair = pl.ds(2 * half, 2)
            lhs = t1[pair].reshape(2 * TOK, NZ * COL)
            out = lax.dot_general(lhs, block, nt, preferred_element_type=F32)
            out = out.reshape(2, TOK, UNIT)
            weighted = out * ha[pair, u].astype(F32)
            score_acc[pair] += weighted[:, :, :128] + weighted[:, :, 128:]
            if where is None:
                cs[u] = out.astype(BF16)
                send(core_copy(u))
            else:
                where[u] = out

    def across_x():
        take(cr, crs.at[0])
        for u in range(NU):
            xs[u] = (pm[u, 1 - xh] + cr[u, 1 - xh].astype(F32)).astype(BF16)
            send(x_copy(u))

    def back_of():
        take(xr, xrs.at[0])
        for u in range(NU):
            bk[u] = pm[u, xh] + cr[u, xh].astype(F32) + xr[u].astype(F32)

    lane = lax.broadcasted_iota(jnp.int32, (1, TOK), 1)

    def mask_row():
        return maskv[...].astype(F32)

    def sum_copy(k, owner):
        return remote(sb.at[owner], sb.at[owner], (sbs, sbr), (0, 0), g_at(k))

    def factor_copy(k, owner):
        return remote(fg.at[owner], fg.at[owner], (fgs, fgr), (0, 0), z_at(k))

    row_to = (
        (2 * (1 - c) + xh, core), (2 * c + 1 - xh, xopp), (2 * (1 - c) + 1 - xh, xopp2)
    )

    def row_copy(j):
        return remote(rb.at[j], rc.at[j], (rbs, rbr), (0, 0), row_to[j][1])

    def score_rows():
        for j in range(3):
            row = jnp.sum(score_acc[row_to[j][0]].T, axis=0, keepdims=True)
            rb[j] = jnp.broadcast_to(row, (8, TOK))
            send(row_copy(j))

    def sums():
        scores = jnp.sum(score_acc[mine].T, axis=0, keepdims=True)
        take(rc, rbr.at[0])
        scores = (scores + rc[0, 0:1, :] + rc[1, 0:1, :] + rc[2, 0:1, :]) * mask_row()
        first_sum = jnp.sum(jnp.where(lane < L, scores, 0.0), axis=1, keepdims=True)
        second_sum = jnp.sum(jnp.where(lane < L, 0.0, scores), axis=1, keepdims=True)
        row = lax.broadcasted_iota(jnp.int32, (8, 128), 0)
        sb[g] = jnp.where(row == 0, first_sum, second_sum)
        for k in range(1, 8):
            send(sum_copy(k, g))

    def factors():
        take(sb.at[pl.ds(0, 7)], sbr.at[0])
        total = sb[0]
        for i in range(1, 8):
            total = total + sb[i]
        count0 = cntv[0].astype(F32)
        count1 = cntv[1].astype(F32)
        reward0 = beta_coef * total[0:1, :] / count0
        reward1 = beta_coef * total[1:2, :] / count1
        margin = reward0 - reward1 - gamma_margin
        weight = jax.nn.sigmoid(-margin) * loss_scale * beta_coef
        factor = jnp.where(lane < L, -weight / count0, weight / count1) * mask_row()
        fg[z] = jnp.broadcast_to(factor, (8, 128))
        for k in range(1, 8):
            send(factor_copy(k, z))
        pair = jnp.maximum(-margin, 0.0) + jnp.log1p(jnp.exp(-jnp.abs(margin)))
        lossv[0] = pair[0, 0]
        out_copies.append(pltpu.make_async_copy(lossv, loss, out_sem.at[3]))
        out_copies[-1].start()

    def grads(first, units):
        by_row = jnp.broadcast_to(fg[z][0:1, :], (TOK, 128)).T
        by_row = jnp.concatenate([by_row, by_row], axis=1)
        for u in range(first, first + units):
            cols = slice(u * UNIT, (u + 1) * UNIT)
            wide = gv[:, cols].astype(F32)
            sig = jax.nn.sigmoid(wide)
            grad = by_row * bk[u]
            swish = wide * sig
            slope = sig + swish * (1.0 - sig)
            gg[:, cols] = (grad * uv[:, cols].astype(F32) * slope).astype(BF16)
            gu[:, cols] = (grad * swish).astype(BF16)

    def scaled():
        take(fg.at[pl.ds(0, 7)], fgr.at[0])

        def scale(i, carry):
            at = pl.ds(pl.multiple_of(i * TOK, TOK), TOK)
            by_lane = fg[i][0:1, :]
            for c_ in range(2):
                t2s[c_, :, at] = (t2t[c_, :, at].astype(F32) * by_lane).astype(BF16)
            return carry

        lax.fori_loop(0, NZ, scale, 0)

    nn = (((1,), (0,)), ((), ()))

    def core_copy2(u):
        return remote(cs2.at[u], cr2.at[u], (css2, crs2), (0, u), core)

    def x_copy2(u):
        return remote(xs2.at[u], xr2.at[u], (xss2, xrs2), (0, u), xopp)

    def product2(u):
        rhs = hg[:, u].reshape(NZ * TOK, UNIT)
        out = lax.dot_general(t2s[1 - c], rhs, nn, preferred_element_type=F32)
        cs2[u] = out.astype(BF16).reshape(2, COL, UNIT)
        send(core_copy2(u))
        out = lax.dot_general(t2s[c], rhs, nn, preferred_element_type=F32)
        dm[u] = out.reshape(2, COL, UNIT)

    def across_x2(u):
        core_copy2(u).wait_recv()
        xs2[u] = (dm[u, 1 - xh] + cr2[u, 1 - xh].astype(F32)).astype(BF16)
        send(x_copy2(u))

    def write(u):
        x_copy2(u).wait_recv()
        rows = pl.ds(u * UNIT, UNIT)
        gd[rows, :] = (dm[u, xh] + cr2[u, xh].astype(F32) + xr2[u].astype(F32)).T

    def flush():
        take(t1.at[pl.ds(0, 3)], t1s.at[0])
        take(t2.at[pl.ds(0, 28), pl.ds(0, 16), :], t2as.at[0])
        take(t2.at[:, pl.ds(0, 112), :], t2gs.at[0])
        take(ha.at[pl.ds(0, 3)], has.at[0])

    def flush_rest():
        take(rb, rbs.at[0])
        take(sb.at[pl.ds(0, 7)], sbs.at[0])
        take(fg.at[pl.ds(0, 7)], fgs.at[0])
        take(cs, css.at[0])
        take(xs, xss.at[0])

    tasks = {
        "W": w_step, "H": h_step, "pass": t2_pass_on, "turn": t2_turn, "t1": t1_wait,
        "P": product, "PX": across_x, "PB": back_of, "sum": sums, "factor": factors, "rows": score_rows, "hid": hidden_pass_on, "hids": hidden_here,
        "grad": grads, "scale": scaled, "D": product2, "DX": across_x2, "DO": write,
        "flush": flush, "rest": flush_rest,
    }
    for name, *given in SCHEDULE:
        tasks[name](*given)

    take(cs2, css2.at[0])
    take(xs2, xss2.at[0])
    for copy in out_copies:
        copy.wait()


def hand_over(*refs):
    sems = refs[-1]
    copies = [pltpu.make_async_copy(refs[i], refs[3 + i], sems.at[i]) for i in range(3)]
    for copy in copies:
        copy.start()
    for copy in copies:
        copy.wait()


def on_device(gate_pre, up_pre, down_weight, residual, target_rows, loss_mask, response_count):
    any_space = pl.BlockSpec(memory_space=pl.ANY)
    vmem = pl.BlockSpec(memory_space=pltpu.VMEM)
    sem = pltpu.SemaphoreType.DMA
    scratch = [
        pltpu.VMEM((TOK, HID), BF16),
        pltpu.VMEM((TOK, HID), BF16),
        pltpu.VMEM((TOK, 512), BF16),
        pltpu.VMEM((TOK, D), BF16),
        pltpu.VMEM((4, TOK, NZ * COL), BF16),
        pltpu.VMEM((4, TOK, NZ * COL), BF16),
        pltpu.VMEM((4 * NZ, TOK, COL), BF16),
        pltpu.VMEM((2, 2 * COL, NZ * TOK), BF16),
        pltpu.VMEM((2, 2 * COL, NZ * TOK), BF16),
        pltpu.VMEM((NZ, HID, COL), BF16),
        pltpu.VMEM((NZ, NU, TOK, UNIT), BF16),
        pltpu.VMEM((NU, 2, TOK, UNIT), F32),
        pltpu.VMEM((NU, 2, TOK, UNIT), BF16),
        pltpu.VMEM((NU, 2, TOK, UNIT), BF16),
        pltpu.VMEM((NU, TOK, UNIT), BF16),
        pltpu.VMEM((NU, TOK, UNIT), BF16),
        pltpu.VMEM((NU, TOK, UNIT), F32),
        pltpu.VMEM((NU, 2, COL, UNIT), F32),
        pltpu.VMEM((NU, 2, COL, UNIT), BF16),
        pltpu.VMEM((NU, 2, COL, UNIT), BF16),
        pltpu.VMEM((NU, COL, UNIT), BF16),
        pltpu.VMEM((NU, COL, UNIT), BF16),
        pltpu.VMEM((8, 8, 128), F32),
        pltpu.VMEM((8, 8, 128), F32),
        pltpu.VMEM((4, TOK, 128), F32),
        pltpu.VMEM((4, NU, TOK, UNIT), BF16),
        pltpu.VMEM((3, 8, TOK), F32),
        pltpu.VMEM((3, 8, TOK), F32),
        pltpu.VMEM((1, TOK), jnp.int32),
        pltpu.SMEM((2,), jnp.int32),
        pltpu.SMEM((1,), F32),
        sem((7,)),
        sem((4,)),
        sem((2, len(W_GROUPS))),
        sem((2, STEPS, len(W_GROUPS))),
        sem((2, len(H_GROUPS))),
        sem((2, STEPS, len(H_GROUPS))),
        *[sem((1,)) for _ in range(6)],
        *[sem((1,)) for _ in range(5)],
        sem((NU,)),
        sem((1,)),
        sem((NU,)),
        *[sem((1,)) for _ in range(4)],
        sem((1,)),
        sem((3,)),
        *[sem((1,)) for _ in range(2)],
    ]
    macs = 2 * 4 * TOK * NZ * COL * HID
    loss, grad_gate, grad_up, grad_down = pl.pallas_call(
        kernel,
        out_shape=(
            jax.ShapeDtypeStruct((1,), F32),
            pltpu.VMEM(gate_pre.shape, BF16),
            pltpu.VMEM(gate_pre.shape, BF16),
            pltpu.VMEM(down_weight.shape, F32),
        ),
        in_specs=[any_space] * 7,
        out_specs=(any_space, vmem, vmem, vmem),
        scratch_shapes=scratch,
        compiler_params=pltpu.CompilerParams(
            collective_id=0, has_side_effects=True, vmem_limit_bytes=56 << 20
        ),
        cost_estimate=pl.CostEstimate(flops=2 * macs, bytes_accessed=6 << 20, transcendentals=0),
    )(
        gate_pre, up_pre, down_weight, residual, target_rows,
        loss_mask.reshape(1, TOK), response_count,
    )
    grad_gate, grad_up, grad_down = pl.pallas_call(
        hand_over,
        out_shape=(
            jax.ShapeDtypeStruct(gate_pre.shape, BF16),
            jax.ShapeDtypeStruct(gate_pre.shape, BF16),
            jax.ShapeDtypeStruct(down_weight.shape, F32),
        ),
        in_specs=[vmem] * 3,
        out_specs=(any_space,) * 3,
        scratch_shapes=[sem((3,))],
    )(*[pltpu.with_memory_space_constraint(a, pltpu.VMEM) for a in (grad_gate, grad_up, grad_down)])
    return loss, grad_gate, grad_up, grad_down


def solution(mesh):
    placed = (
        P("fsdp", "tensor"),
        P("fsdp", "tensor"),
        P("tensor", "fsdp"),
        P("fsdp", None),
        P("fsdp", None),
        P("fsdp"),
        P("fsdp"),
    )
    return jax.shard_map(
        on_device,
        mesh=mesh,
        in_specs=placed,
        out_specs=(P("fsdp"), P("fsdp", "tensor"), P("fsdp", "tensor"), P("tensor", "fsdp")),
        check_vma=False,
    )
```
